32 devices in a mesh: dp: 4 (over y, x), vocab: 8 (over z, core).
Axes of the slice: x: 2, y: 2, z: 4, core: 2. Of those that a mesh axis runs over, the one named last changes fastest.
Arguments:
- hidden: bfloat16 [768, 5120], P('dp', 'vocab'), may hold values from -128 to 128
- head: bfloat16 [7168, 5120], P('vocab', 'dp'), may hold values from -0.125 to 0.125
- targets: int32 [4, 192], P('dp'), may hold values from 0 to 7167
- segments: int32 [4, 192], P('dp'), may hold values from 0 to 15, never falling along the last dimension, each value on 1 to 32 neighbouring positions
- loss_mask: int32 [4, 192], P('dp'), may hold values 0 or 1
Outputs:
- grad_hidden: bfloat16 [768, 5120], P('dp', 'vocab')
- grad_head: bfloat16 [7168, 5120], P('vocab', 'dp')
The draws below stay inside these ranges and needn't reach their ends.
All inputs are finite; a program needn't handle non-finite values. No bound on the sum of `loss_mask` on one device may be relied on, other than what follows from the above.
Results may differ from the reference program's by a relative error of at most 0.0055.
Values may be sent and summed in bfloat16 or wider, within the bound.
A program may use at most 64 MiB of HBM per device.

```python
import math
import jax
import jax.numpy as jnp
import numpy as np

D = 5120
TOK = 192
SEGS = 16
MOST = 32
VOCAB = 7168
GROUPS = 4
TOKENS = 768


def draw_rows(key, shape, half):
    return jax.random.uniform(key, shape, jnp.float32, -half, half)


def head_values(key, half):
    return draw_rows(key, (VOCAB, D), half)


def draw_head(key, part):
    shared = head_values(key, 0.125)
    return shared.astype(jnp.bfloat16)


def align_rows(values, shared, keys, half):
    count = min(8, TOKENS // 2)
    picked = jax.random.permutation(keys[2], TOKENS)[:2 * count]
    first = jax.random.randint(keys[3], (count,), 0, VOCAB)
    second = jax.random.randint(keys[4], (count,), 0, VOCAB)
    strength = jnp.array([4.0, 8.0, 12.0, 4.0, 8.0, 12.0, 8.0, 12.0], jnp.float32)[:count]
    factor = strength
    aligned = factor[:, None] * (shared[first] + shared[second])
    fresh = draw_rows(keys[5], (2, count, D), half)
    decoys = factor[:, None] * (fresh[0] + fresh[1])
    values = values.at[picked[:count]].set(aligned)
    return values.at[picked[count:]].set(decoys)


def draw_hidden(key, part):
    half = 0.125
    shared = head_values(key, half)
    key = jax.random.fold_in(key, 7)
    keys = jax.random.split(key, 6)
    values = jnp.clip(jax.random.normal(keys[1], (TOKENS, D), jnp.float32), -4.0, 4.0)
    values = align_rows(values, shared, keys, half)
    return values.astype(jnp.bfloat16)


def set_ends(drawn, rng, least, high):
    longest = drawn.shape.index(max(drawn.shape))
    spots = []
    for shift in (0, 1):
        where = [jax.random.randint(jax.random.fold_in(rng, axis), (), 0, length) for axis, length in enumerate(drawn.shape)]
        where[longest] = (where[longest] + shift) % drawn.shape[longest]
        spots.append(tuple(where))
    return drawn.at[spots[0]].set(least).at[spots[1]].set(high)


def cumulative_ranks(amount, skew):
    loads = [(1 << 20) // math.isqrt(standing ** skew) + 1 for standing in range(1, amount + 1)]
    deviation = 1 + sum(loads) // (1 << 30)
    return np.cumsum(np.array([max(1, weight // deviation) for weight in loads]))


def ranked(key, shape, number_of, slope):
    listing = cumulative_ranks(number_of, slope)
    ticket = jax.random.randint(jax.random.fold_in(key, 1), shape, 0, int(listing[number_of - 1]))
    standing = jnp.searchsorted(jnp.asarray(listing, jnp.int32), ticket, side="right")
    return jax.random.permutation(jax.random.fold_in(key, 2), number_of)[standing].astype(jnp.int32)


def profile(amount, total, bound, skew):
    weights = [(1 << 20) // math.isqrt(standing ** skew) + 1 for standing in range(2, amount + 1)]
    rest, given = total - bound - (amount - 1), [1] * (amount - 1)
    while rest > 0:
        free = [i for i in range(amount - 1) if given[i] < bound]
        mass, budget = sum([weights[i] for i in free]), rest
        for i in free:
            addition = min(bound - given[i], max(1, budget * weights[i] // mass), rest)
            given[i] = given[i] + addition
            rest = rest - addition
    return np.array([bound] + given)


def uneven_parts(own_key, amount, total, limit, skew):
    if amount == 2:
        one = jax.random.randint(own_key, (), max(1, total - limit), min(limit, total - 1) + 1)
        return jnp.stack([one, total - one])
    lengths = jnp.asarray(profile(amount, total, limit, skew), jnp.int32)
    pairs = (amount - 1) // 2
    donor, receiver = lengths[1:1 + 2 * pairs:2], lengths[2:2 + 2 * pairs:2]
    margin = jnp.minimum(donor - 1, limit - receiver)
    passed = jax.random.randint(jax.random.fold_in(own_key, 1), (pairs,), 0, 1 << 20) % (margin + 1)
    lengths = lengths.at[1:1 + 2 * pairs:2].set(donor - passed).at[2:2 + 2 * pairs:2].set(receiver + passed)
    return lengths[jax.random.permutation(jax.random.fold_in(own_key, 2), amount)]


def setup_inputs(seed: int = 0) -> dict:
    arg_keys = jax.random.split(jax.random.key(seed), 6)
    hidden = draw_hidden(jax.random.fold_in(arg_keys[5], 71), 0)
    head = draw_head(jax.random.fold_in(arg_keys[5], 71), 0)
    targets = set_ends(ranked(arg_keys[2], (GROUPS, TOK), VOCAB, 2), jax.random.fold_in(arg_keys[2], 3), 0, VOCAB - 1).astype(jnp.int32)
    segments = jax.vmap(lambda own: jnp.searchsorted(jnp.cumsum(uneven_parts(own, SEGS, TOK, MOST, 2)), jnp.arange(TOK), side="right"))(jax.random.split(arg_keys[3], GROUPS)).reshape((GROUPS, TOK)).astype(jnp.int32)
    loss_mask = set_ends((jax.random.randint(arg_keys[4], (GROUPS, TOK), 0, 4) < 3).astype(jnp.int32), jax.random.fold_in(arg_keys[4], 1), 0, 1)
    return dict(hidden=hidden, head=head, targets=targets, segments=segments, loss_mask=loss_mask)


loss_scale = 256.0


def reference(hidden, head, targets, segments, loss_mask):
    logits = jnp.dot(hidden, head.T, preferred_element_type=jnp.float32)
    row_max = jnp.max(logits, axis=1, keepdims=True)
    log_norm = row_max + jnp.log(jnp.sum(jnp.exp(logits - row_max), axis=1, keepdims=True))
    mask_f = loss_mask.astype(jnp.float32)
    same = (segments[:, :, None] == segments[:, None, :]).astype(jnp.float32)
    counts = jnp.einsum("gij,gj->gi", same, mask_f)
    weight = (loss_scale * mask_f / jnp.maximum(counts, 1.0)).reshape(-1)
    columns = jnp.arange(VOCAB, dtype=jnp.int32)
    onehot = (targets.reshape(-1)[:, None] == columns[None, :]).astype(jnp.float32)
    grad_logits = (weight[:, None] * (jnp.exp(logits - log_norm) - onehot)).astype(jnp.bfloat16)
    grad_hidden = jnp.dot(grad_logits, head, preferred_element_type=jnp.float32).astype(jnp.bfloat16)
    grad_head = jnp.dot(grad_logits.T, hidden, preferred_element_type=jnp.float32).astype(jnp.bfloat16)
    return grad_hidden, grad_head
```

```python
import functools

import jax
import jax.numpy as jnp
from jax import lax
from jax.experimental import pallas as pl
from jax.experimental.pallas import tpu as pltpu
from jax.sharding import PartitionSpec as P

loss_scale = 256.0
MESH = pl.DeviceIdType.MESH
CHUNKS = 2


def token_weight(segments, loss_mask):
    mask_f = loss_mask[0].astype(jnp.float32)
    seg_ids = segments[0]
    same = (seg_ids[:, None] == seg_ids[None, :]).astype(jnp.float32)
    counts = jnp.sum(same * mask_f[None, :], axis=1)
    return loss_scale * mask_f / jnp.maximum(counts, 1.0)


def kernel(
    rows, width, vocab_rows,
    hidden_ref, head_hbm, target_ref, weight_ref,
    out_hidden, out_head,
    head, feats, mine, part, recv_a, recv_b, tile, stats, grads,
    q_keep, q_pair, q_pair_in, q_plane, q_plane_in, q_line, ghead,
    head_sem, out_sem, own_sem,
    line_s, line_r, plane_s, plane_r, pair_s, pair_r,
    red_s, red_r, stat_s, stat_r, gat_s, gat_r,
    qpair_s, qpair_r, qplane_s, qplane_r, qline_s, qline_r,
):
    g = lax.axis_index("dp")
    v = lax.axis_index("vocab")
    z, c = v // 2, v % 2
    gy, gx = g // 2, g % 2
    xn, yn, dn = gy * 2 + 1 - gx, (1 - gy) * 2 + gx, (1 - gy) * 2 + 1 - gx
    sib = z * 2 + 1 - c
    half = rows // 2
    col = pl.multiple_of(c * width, 128)
    other_col = pl.multiple_of((1 - c) * width, 128)
    sends = []

    def remote(src, dst, ssem, rsem, dev):
        return pltpu.make_async_remote_copy(
            src_ref=src, dst_ref=dst, send_sem=ssem, recv_sem=rsem,
            device_id=dev, device_id_type=MESH,
        )

    def bin_rows(b, off=0, n=None):
        n = rows if n is None else n
        return pl.ds(pl.multiple_of(b * rows + off, 16), n)

    head_copy = pltpu.make_async_copy(head_hbm, head, head_sem)
    head_copy.start()

    barrier = pltpu.get_barrier_semaphore()
    for p in (xn, yn, dn):
        pl.semaphore_signal(barrier, inc=1, device_id=(p, v), device_id_type=MESH)
    for i in range(1, 8):
        pl.semaphore_signal(barrier, inc=1, device_id=(g, lax.rem(v + i, 8)), device_id_type=MESH)
    for k in range(CHUNKS):
        feats[k, z] = hidden_ref[k * rows:(k + 1) * rows, :]
    tile[...] = jnp.ones_like(tile)
    pl.semaphore_wait(barrier, 10)

    def line_copy(k, right, d):
        step = 1 if right else -1
        s = z - step * d
        return remote(
            feats.at[k, s], feats.at[k, s], line_s.at[k, int(right), d], line_r.at[k, int(right), d],
            (g, (z + step) * 2 + c),
        )

    def line_ok(right, d):
        if right:
            return (z >= d) & (z < 3)
        return (z + d <= 3) & (z > 0)

    def line_send(k, right, d):
        @pl.when(line_ok(right, d))
        def _():
            line_copy(k, right, d).start()

    def line_send_wait(k, right, d):
        @pl.when(line_ok(right, d))
        def _():
            line_copy(k, right, d).wait_send()

    def plane_copy(k, s):
        return remote(
            feats.at[k, s], mine.at[k, bin_rows(g), pl.ds(col, width)],
            plane_s.at[k, s], plane_r.at[k, g], (s, v),
        )

    def own_copy(k):
        return pltpu.make_async_copy(
            feats.at[k, g], mine.at[k, bin_rows(g), pl.ds(col, width)], own_sem.at[k]
        )

    def plane_send(k, s):
        @pl.when(s == g)
        def _():
            own_copy(k).start()

        @pl.when(s != g)
        def _():
            plane_copy(k, s).start()

    def line_recv(k, right, d):
        step = 1 if right else -1
        s = z - step * d
        here = (z >= d) if right else (z + d <= 3)

        @pl.when(here)
        def _():
            remote(
                feats.at[k, s], feats.at[k, s], line_s.at[k, int(right), d - 1],
                line_r.at[k, int(right), d - 1], (g, v),
            ).wait_recv()
            if d < 3:
                line_send(k, right, d)
            plane_send(k, s)

    def pair_copy(k, b):
        at = mine.at[k, bin_rows(b), pl.ds(col, width)]
        return remote(at, at, pair_s.at[k, b], pair_r.at[k, b], (g, sib))

    def hidden_line(k):
        for d in (1, 2, 3):
            line_recv(k, True, d)
            line_recv(k, False, d)

    def hidden_plane(k):
        own_copy(k).wait()
        pair_copy(k, g).start()
        for p in (xn, yn, dn):
            at = mine.at[k, bin_rows(p), pl.ds(col, width)]
            remote(at, at, plane_s.at[k, p], plane_r.at[k, p], (p, v)).wait_recv()
            pair_copy(k, p).start()
        for p in (g, xn, yn, dn):
            at = mine.at[k, bin_rows(p), pl.ds(other_col, width)]
            remote(at, at, pair_s.at[k, p], pair_r.at[k, p], (g, sib)).wait_recv()

    def hidden_finish(k):
        for right in (True, False):
            for d in (0, 1, 2):
                line_send_wait(k, right, d)
        for s in range(4):
            @pl.when(s != g)
            def _():
                plane_copy(k, s).wait_send()
        for p in (g, xn, yn, dn):
            pair_copy(k, p).wait_send()

    def red_copy(k, way, i):
        buf = (recv_a, recv_b)[way]
        off = way * half
        first, second = ((xn, yn), (yn, xn))[way]
        b = (dn, first, second)[i]
        dev = (first, first, second)[i]
        return remote(
            part.at[k, bin_rows(b, off, half)], buf.at[k, i],
            red_s.at[k, way, i], red_r.at[k, way, i], (dev, v),
        )

    def logits_start(k):
        part[k] = lax.dot_general(
            mine[k], head[...], (((1,), (1,)), ((), ())), preferred_element_type=jnp.float32
        )
        for i in (0, 1):
            for way in (0, 1):
                red_copy(k, way, i).start()

    def logits_forward(k):
        for way in (0, 1):
            buf = (recv_a, recv_b)[way]
            second = (yn, xn)[way]
            red_copy(k, way, 0).wait_recv()
            at = bin_rows(second, way * half, half)
            part[k, at] = part[k, at] + buf[k, 0]
            red_copy(k, way, 2).start()

    def stat_copy(k, i):
        peer = lax.rem(v + i, 8)
        return remote(stats.at[k, v], stats.at[k, v], stat_s.at[k, i - 1], stat_r.at[k, i - 1], (g, peer))

    def logits_finish(k):
        for i in (1, 2):
            for way in (0, 1):
                red_copy(k, way, i).wait_recv()
        for way in (0, 1):
            buf = (recv_a, recv_b)[way]
            at = bin_rows(g, way * half, half)
            part[k, at] = part[k, at] + buf[k, 1] + buf[k, 2]
        logits = part[k, bin_rows(g)]
        top = jnp.max(logits, axis=1, keepdims=True)
        total = jnp.sum(jnp.exp(logits - top), axis=1, keepdims=True)
        lane = lax.broadcasted_iota(jnp.int32, (rows, 128), 1)
        tile[0:rows, :] = jnp.where(lane == 0, top, total)
        stats[k, v] = tile[...].T[0:8, :]
        for i in range(1, 8):
            stat_copy(k, i).start()

    def gat_copy(k, to_y, i):
        dev = yn if to_y else xn
        if i == 2:
            b, off = (xn, 0) if to_y else (yn, half)
        else:
            b, off = g, ((half, 0) if to_y else (0, half))[i]
        at = grads.at[k, bin_rows(b, off, half)]
        return remote(at, at, gat_s.at[k, int(to_y), i], gat_r.at[k, int(to_y), i], (dev, v))

    def gat_wait(k, to_y, i):
        gat_copy(k, to_y, i).wait_recv()

    def grads_start(k):
        for i in range(1, 8):
            stat_copy(k, i).wait_recv()
        tops = stats[k, :, 0, :]
        totals = stats[k, :, 1, :]
        top = jnp.max(tops, axis=0, keepdims=True)
        total = jnp.sum(totals * jnp.exp(tops - top), axis=0, keepdims=True)
        norm = jnp.broadcast_to(top + jnp.log(total), (128, 128)).T[0:rows, 0:1]
        logits = part[k, bin_rows(g)]
        weight = weight_ref[k * rows:(k + 1) * rows, :]
        target = target_ref[k * rows:(k + 1) * rows, :] - v * vocab_rows
        columns = lax.broadcasted_iota(jnp.int32, (rows, vocab_rows), 1)
        onehot = (target == columns).astype(jnp.float32)
        grads[k, bin_rows(g)] = (weight * (jnp.exp(logits - norm) - onehot)).astype(jnp.bfloat16)
        for i in (0, 1):
            for to_y in (False, True):
                gat_copy(k, to_y, i).start()

    def grads_forward(k):
        gat_wait(k, False, 0)
        gat_copy(k, True, 2).start()
        gat_wait(k, True, 0)
        gat_copy(k, False, 2).start()

    def qpair_copy(k, b):
        return remote(q_pair.at[k, b], q_pair_in.at[k, b], qpair_s.at[k, b], qpair_r.at[k, b], (g, sib))

    def qplane_copy(k, b):
        return remote(q_plane.at[k, b], q_plane_in.at[k, g], qplane_s.at[k, b], qplane_r.at[k, g], (b, v))

    def qline_copy(k, s):
        return remote(
            q_plane_in.at[k, s], q_line.at[k, z], qline_s.at[k, s], qline_r.at[k, z], (g, s * 2 + c)
        )

    def terms_start(k, b):
        grad = grads[k, bin_rows(b)]
        q_pair[k, b] = jnp.dot(
            grad, head[:, pl.ds(other_col, width)], preferred_element_type=jnp.float32
        ).astype(jnp.bfloat16)
        qpair_copy(k, b).start()
        q_keep[k, b] = jnp.dot(grad, head[:, pl.ds(col, width)], preferred_element_type=jnp.float32)

    def line_start(k, s):
        @pl.when(s == z)
        def _():
            q_line[k, z] = q_plane_in[k, s]

        @pl.when(s != z)
        def _():
            qline_copy(k, s).start()

    def terms_send(k, b, own):
        qpair_copy(k, b).wait_recv()
        total = (q_keep[k, b] + q_pair_in[k, b].astype(jnp.float32)).astype(jnp.bfloat16)
        if own:
            q_plane_in[k, b] = total
            line_start(k, b)
        else:
            q_plane[k, b] = total
            qplane_copy(k, b).start()

    def terms_line(k):
        for p in (xn, yn, dn):
            remote(q_plane.at[k, p], q_plane_in.at[k, p], qplane_s.at[k, p], qplane_r.at[k, p], (p, v)).wait_recv()
            line_start(k, p)

    def terms_finish(k):
        for s in range(4):
            @pl.when(s != z)
            def _():
                remote(q_line.at[k, s], q_line.at[k, s], qline_s.at[k, s], qline_r.at[k, s], (g, v)).wait_recv()
        total = q_line[k, 0].astype(jnp.float32)
        for s in range(1, 4):
            total = total + q_line[k, s].astype(jnp.float32)
        out_hidden[k * rows:(k + 1) * rows, :] = total.astype(jnp.bfloat16)

    def terms_round(k):
        terms_start(k, g)
        gat_wait(k, False, 1)
        terms_start(k, xn)
        terms_send(k, g, True)
        gat_wait(k, True, 1)
        terms_start(k, yn)
        terms_send(k, xn, False)
        gat_wait(k, False, 2)
        gat_wait(k, True, 2)
        terms_start(k, dn)
        terms_send(k, yn, False)
        terms_send(k, dn, False)

    for k in range(CHUNKS):
        line_send(k, True, 0)
        line_send(k, False, 0)
        plane_send(k, z)
    hidden_line(0)
    hidden_plane(0)
    head_copy.wait()
    logits_start(0)
    hidden_line(1)
    hidden_plane(1)
    logits_start(1)
    logits_forward(0)
    logits_forward(1)
    logits_finish(0)
    grads_start(0)
    logits_finish(1)
    grads_forward(0)
    grads_start(1)
    terms_round(0)
    grads_forward(1)
    terms_line(0)
    terms_round(1)
    terms_line(1)

    tiles = 4
    tile_cols = ghead.shape[1] // tiles
    outs = []
    for n in range(tiles):
        at = pl.ds(n * tile_cols, tile_cols)
        total = None
        for k in range(CHUNKS):
            term = lax.dot_general(
                grads[k], mine[k, :, at], (((0,), (0,)), ((), ())), preferred_element_type=jnp.float32
            )
            total = term if total is None else total + term
        ghead[:, at] = total.astype(jnp.bfloat16)
    out_copy = pltpu.make_async_copy(ghead, out_head, out_sem)
    out_copy.start()

    for k in range(CHUNKS):
        terms_finish(k)
    for k in range(CHUNKS):
        hidden_finish(k)
        for way in (0, 1):
            for i in (0, 1, 2):
                red_copy(k, way, i).wait_send()
                gat_copy(k, way, i).wait_send()
        for i in range(1, 8):
            stat_copy(k, i).wait_send()
        for p in (g, xn, yn, dn):
            qpair_copy(k, p).wait_send()
        for p in (xn, yn, dn):
            qplane_copy(k, p).wait_send()
        for s in range(4):
            @pl.when(s != z)
            def _():
                qline_copy(k, s).wait_send()
    out_copy.wait()


def fused(hidden, head, targets, segments, loss_mask):
    tokens, width = hidden.shape
    vocab_rows, head_width = head.shape
    rows = tokens // CHUNKS
    half = rows // 2
    weight = token_weight(segments, loss_mask)[:, None]
    target = targets[0][:, None]
    bf16, f32 = jnp.bfloat16, jnp.float32
    dma = pltpu.SemaphoreType.DMA
    vmem = pl.BlockSpec(memory_space=pltpu.VMEM)
    hbm = pl.BlockSpec(memory_space=pl.ANY)
    K = CHUNKS
    return pl.pallas_call(
        functools.partial(kernel, rows, width, vocab_rows),
        out_shape=(
            jax.ShapeDtypeStruct(hidden.shape, bf16),
            jax.ShapeDtypeStruct(head.shape, bf16),
        ),
        in_specs=[vmem, hbm, vmem, vmem],
        out_specs=(vmem, hbm),
        scratch_shapes=[
            pltpu.VMEM(head.shape, bf16),
            pltpu.VMEM((K, 4, rows, width), bf16),
            pltpu.VMEM((K, 4 * rows, head_width), bf16),
            pltpu.VMEM((K, 4 * rows, vocab_rows), f32),
            pltpu.VMEM((K, 3, half, vocab_rows), f32),
            pltpu.VMEM((K, 3, half, vocab_rows), f32),
            pltpu.VMEM((128, 128), f32),
            pltpu.VMEM((K, 8, 8, 128), f32),
            pltpu.VMEM((K, 4 * rows, vocab_rows), bf16),
            pltpu.VMEM((K, 4, rows, width), f32),
            pltpu.VMEM((K, 4, rows, width), bf16),
            pltpu.VMEM((K, 4, rows, width), bf16),
            pltpu.VMEM((K, 4, rows, width), bf16),
            pltpu.VMEM((K, 4, rows, width), bf16),
            pltpu.VMEM((K, 4, rows, width), bf16),
            pltpu.VMEM(head.shape, bf16),
            dma, dma, dma((K,)),
            dma((K, 2, 3)), dma((K, 2, 3)),
            dma((K, 4)), dma((K, 4)), dma((K, 4)), dma((K, 4)),
            dma((K, 2, 3)), dma((K, 2, 3)),
            dma((K, 7)), dma((K, 7)),
            dma((K, 2, 3)), dma((K, 2, 3)),
            dma((K, 4)), dma((K, 4)), dma((K, 4)), dma((K, 4)), dma((K, 4)), dma((K, 4)),
        ],
        compiler_params=pltpu.CompilerParams(
            collective_id=0, has_side_effects=True, vmem_limit_bytes=56 * 1024 * 1024
        ),
        cost_estimate=pl.CostEstimate(
            flops=3 * 2 * 4 * tokens * vocab_rows * head_width,
            bytes_accessed=4 * vocab_rows * head_width,
            transcendentals=2 * tokens * vocab_rows,
        ),
    )(hidden, head, target, weight)


def body(hidden, head, targets, segments, loss_mask):
    vocab_rows = head.shape[0]
    features = lax.all_gather(hidden, "vocab", axis=1, tiled=True)
    wide_head = lax.all_gather(head, "dp", axis=1, tiled=True)
    logits = lax.dot_general(
        features, wide_head, (((1,), (1,)), ((), ())), preferred_element_type=jnp.float32
    )
    local_max = jnp.max(logits, axis=1)
    row_max = lax.pmax(local_max, "vocab")
    row_total = lax.psum(jnp.sum(jnp.exp(logits - row_max[:, None]), axis=1), "vocab")
    log_norm = row_max + jnp.log(row_total)
    weight = token_weight(segments, loss_mask)
    vocab_start = lax.axis_index("vocab") * vocab_rows
    columns = vocab_start + lax.broadcasted_iota(jnp.int32, (1, vocab_rows), 1)
    onehot = (targets[0][:, None] == columns).astype(jnp.float32)
    grad_logits = (weight[:, None] * (jnp.exp(logits - log_norm[:, None]) - onehot)).astype(
        jnp.bfloat16
    )
    partial_terms = jnp.dot(grad_logits, wide_head, preferred_element_type=jnp.float32)
    grad_hidden = lax.psum_scatter(partial_terms, "vocab", scatter_dimension=1, tiled=True).astype(
        jnp.bfloat16
    )
    group_cols = lax.all_to_all(features, "dp", split_axis=1, concat_axis=0, tiled=True)
    head_total = lax.dot_general(
        lax.all_gather(grad_logits, "dp", axis=0, tiled=True),
        group_cols,
        (((0,), (0,)), ((), ())),
        preferred_element_type=jnp.float32,
    )
    return (grad_hidden, head_total.astype(jnp.bfloat16))


def solution(mesh):
    placed = (P("dp", "vocab"), P("vocab", "dp"), P("dp", None), P("dp", None), P("dp", None))
    fits = mesh.shape["dp"] == 4 and mesh.shape["vocab"] == 8
    return jax.shard_map(
        fused if fits else body,
        mesh=mesh,
        in_specs=placed,
        out_specs=(P("dp", "vocab"), P("vocab", "dp")),
        check_vma=False,
    )
```

```python
import functools

import jax
import jax.numpy as jnp
from jax import lax
from jax.experimental import pallas as pl
from jax.experimental.pallas import tpu as pltpu
from jax.sharding import PartitionSpec as P

loss_scale = 256.0
MESH = pl.DeviceIdType.MESH
CHUNKS = 3


def token_weight(segments, loss_mask):
    mask_f = loss_mask[0].astype(jnp.float32)
    seg_ids = segments[0]
    same = (seg_ids[:, None] == seg_ids[None, :]).astype(jnp.float32)
    counts = jnp.sum(same * mask_f[None, :], axis=1)
    return loss_scale * mask_f / jnp.maximum(counts, 1.0)


def kernel(
    rows, width, vocab_rows,
    hidden_hbm, head_hbm, target_ref, segment_ref, mask_ref,
    out_hidden, out_head,
    head, feats, mine, part, recv_a, recv_b, tile, stats, grads, weights, target_col,
    q_keep, q_pair, q_pair_in, q_plane, q_plane_in, q_line, ghead,
    head_sem, out_sem, hidden_sem, own_sem,
    line_s, line_r, plane_s, plane_r, pair_s, pair_r,
    red_s, red_r, stat_s, stat_r, gat_s, gat_r,
    qpair_s, qpair_r, qplane_s, qplane_r, qline_s, qline_r,
):
    g = lax.axis_index("dp")
    v = lax.axis_index("vocab")
    z, c = v // 2, v % 2
    gy, gx = g // 2, g % 2
    xn, yn, dn = gy * 2 + 1 - gx, (1 - gy) * 2 + gx, (1 - gy) * 2 + 1 - gx
    peers = (g, xn, yn, dn)
    sib = z * 2 + 1 - c
    half = rows // 2
    col = pl.multiple_of(c * width, 128)
    other_col = pl.multiple_of((1 - c) * width, 128)
    f32, bf16 = jnp.float32, jnp.bfloat16

    def remote(src, dst, ssem, rsem, dev):
        return pltpu.make_async_remote_copy(
            src_ref=src, dst_ref=dst, send_sem=ssem, recv_sem=rsem,
            device_id=dev, device_id_type=MESH,
        )

    def place(r, off=0, n=None):
        return pl.ds(r * rows + off, rows if n is None else n)

    def hidden_copy(k):
        return pltpu.make_async_copy(
            hidden_hbm.at[pl.ds(k * rows, rows)], feats.at[k, z], hidden_sem.at[k]
        )

    for k in range(CHUNKS):
        hidden_copy(k).start()
    head_copy = pltpu.make_async_copy(head_hbm, head, head_sem)
    head_copy.start()

    barrier = pltpu.get_barrier_semaphore()
    for p in (xn, yn, dn):
        pl.semaphore_signal(barrier, inc=1, device_id=(p, v), device_id_type=MESH)
    for i in range(1, 8):
        pl.semaphore_signal(barrier, inc=1, device_id=(g, lax.rem(v + i, 8)), device_id_type=MESH)
    tile[...] = jnp.ones_like(tile)
    for k in range(CHUNKS):
        hidden_copy(k).wait()
    pl.semaphore_wait(barrier, 10)

    def line_copy(k, right, d):
        step = 1 if right else -1
        s = z - step * d
        return remote(
            feats.at[k, s], feats.at[k, s], line_s.at[k, int(right), d], line_r.at[k, int(right), d],
            (g, (z + step) * 2 + c),
        )

    def line_ok(right, d):
        if right:
            return (z >= d) & (z < 3)
        return (z + d <= 3) & (z > 0)

    def line_send(k, right, d):
        @pl.when(line_ok(right, d))
        def _():
            line_copy(k, right, d).start()

    def line_send_wait(k, right, d):
        @pl.when(line_ok(right, d))
        def _():
            line_copy(k, right, d).wait_send()

    def plane_copy(k, s):
        r = (gx + s) % 2 + 2 * ((gy + s // 2) % 2)
        at = pl.ds(pl.multiple_of(r * rows, 16), rows)
        return remote(
            feats.at[k, s], mine.at[k, at, pl.ds(col, width)], plane_s.at[k, s], plane_r.at[k, r], (s, v)
        )

    def own_copy(k):
        return pltpu.make_async_copy(feats.at[k, g], mine.at[k, place(0), pl.ds(col, width)], own_sem.at[k])

    def plane_send(k, s):
        @pl.when(s == g)
        def _():
            own_copy(k).start()

        @pl.when(s != g)
        def _():
            plane_copy(k, s).start()

    def line_recv(k, right, d):
        step = 1 if right else -1
        s = z - step * d
        here = (z >= d) if right else (z + d <= 3)

        @pl.when(here)
        def _():
            remote(
                feats.at[k, s], feats.at[k, s], line_s.at[k, int(right), d - 1],
                line_r.at[k, int(right), d - 1], (g, v),
            ).wait_recv()
            if d < 3:
                line_send(k, right, d)
            plane_send(k, s)

    def pair_copy(k, r):
        at = mine.at[k, place(r), pl.ds(col, width)]
        return remote(at, at, pair_s.at[k, r], pair_r.at[k, r], (g, sib))

    def hidden_first(k):
        line_send(k, True, 0)
        line_send(k, False, 0)
        plane_send(k, z)

    def hidden_line(k):
        for d in (1, 2, 3):
            line_recv(k, True, d)
            line_recv(k, False, d)

    def hidden_plane(k):
        own_copy(k).wait()
        pair_copy(k, 0).start()
        for r in (1, 2, 3):
            at = mine.at[k, place(r), pl.ds(col, width)]
            remote(at, at, plane_s.at[k, r], plane_r.at[k, r], (peers[r], v)).wait_recv()
            pair_copy(k, r).start()
        for r in range(4):
            at = mine.at[k, place(r), pl.ds(other_col, width)]
            remote(at, at, pair_s.at[k, r], pair_r.at[k, r], (g, sib)).wait_recv()

    def hidden_finish(k):
        for right in (True, False):
            for d in (0, 1, 2):
                line_send_wait(k, right, d)
        for s in range(4):
            @pl.when(s != g)
            def _():
                plane_copy(k, s).wait_send()
        for r in range(4):
            pair_copy(k, r).wait_send()

    def red_copy(k, way, i):
        buf = (recv_a, recv_b)[way]
        first, second = ((1, 2), (2, 1))[way]
        r = (3, first, second)[i]
        dev = peers[(first, first, second)[i]]
        return remote(
            part.at[k, place(r, way * half, half)], buf.at[k, i],
            red_s.at[k, way, i], red_r.at[k, way, i], (dev, v),
        )

    def logits_start(k):
        part[k] = lax.dot_general(
            mine[k], head[...], (((1,), (1,)), ((), ())), preferred_element_type=f32
        )
        for i in (0, 1):
            for way in (0, 1):
                red_copy(k, way, i).start()

    def logits_forward(k):
        for way in (0, 1):
            buf = (recv_a, recv_b)[way]
            red_copy(k, way, 0).wait_recv()
            at = place((2, 1)[way], way * half, half)
            part[k, at] = part[k, at] + buf[k, 0]
            red_copy(k, way, 2).start()

    def stat_copy(k, i):
        peer = lax.rem(v + i, 8)
        return remote(stats.at[k, v], stats.at[k, v], stat_s.at[k, i - 1], stat_r.at[k, i - 1], (g, peer))

    def logits_finish(k):
        for i in (1, 2):
            for way in (0, 1):
                red_copy(k, way, i).wait_recv()
        for way in (0, 1):
            buf = (recv_a, recv_b)[way]
            at = place(0, way * half, half)
            part[k, at] = part[k, at] + buf[k, 1] + buf[k, 2]
        logits = part[k, place(0)]
        top = jnp.max(logits, axis=1, keepdims=True)
        total = jnp.sum(jnp.exp(logits - top), axis=1, keepdims=True)
        lane = lax.broadcasted_iota(jnp.int32, (rows, 128), 1)
        tile[0:rows, :] = jnp.where(lane == 0, top, total)
        stats[k, v] = tile[...].T[0:8, :]
        for i in range(1, 8):
            stat_copy(k, i).start()

    def gat_copy(k, to_y, i):
        dev = yn if to_y else xn
        if i == 2:
            src, dst, off = (1, 3, 0) if to_y else (2, 3, half)
        else:
            src, dst, off = 0, 2 if to_y else 1, ((half, 0) if to_y else (0, half))[i]
        return remote(
            grads.at[k, place(src, off, half)], grads.at[k, place(dst, off, half)],
            gat_s.at[k, int(to_y), i], gat_r.at[k, int(to_y), i], (dev, v),
        )

    def gat_wait(k, to_y, i):
        gat_copy(k, to_y, i).wait_recv()

    def grads_start(k):
        for i in range(1, 8):
            stat_copy(k, i).wait_recv()
        tops = stats[k, :, 0, :]
        totals = stats[k, :, 1, :]
        top = jnp.max(tops, axis=0, keepdims=True)
        total = jnp.sum(totals * jnp.exp(tops - top), axis=0, keepdims=True)
        norm = jnp.broadcast_to(top + jnp.log(total), (128, 128)).T[0:rows, 0:1]
        logits = part[k, place(0)]
        weight = weights[k * rows:(k + 1) * rows, :]
        target = target_col[k * rows:(k + 1) * rows, :]
        columns = v * vocab_rows + lax.broadcasted_iota(jnp.int32, (rows, vocab_rows), 1)
        onehot = (target == columns.astype(f32)).astype(f32)
        grads[k, place(0)] = (weight * (jnp.exp(logits - norm) - onehot)).astype(bf16)
        for i in (0, 1):
            for to_y in (False, True):
                gat_copy(k, to_y, i).start()

    def grads_forward(k):
        gat_wait(k, False, 0)
        gat_copy(k, True, 2).start()
        gat_wait(k, True, 0)
        gat_copy(k, False, 2).start()

    def qpair_copy(k, r, n):
        at = pl.ds(r * rows, n * rows)
        return remote(q_pair.at[k, at], q_pair_in.at[k, at], qpair_s.at[k, r], qpair_r.at[k, r], (g, sib))

    def qplane_copy(k, r):
        return remote(
            q_plane.at[k, place(r)], q_plane_in.at[k, place(r)], qplane_s.at[k, r], qplane_r.at[k, r], (peers[r], v)
        )

    def qline_copy(k, r):
        s = peers[r]
        return remote(
            q_plane_in.at[k, place(r)], q_line.at[k, z], qline_s.at[k, r], qline_r.at[k, z], (g, s * 2 + c)
        )

    def terms_start(k, r, n=1):
        at = pl.ds(r * rows, n * rows)
        grad = grads[k, at]
        q_pair[k, at] = jnp.dot(
            grad, head[:, pl.ds(other_col, width)], preferred_element_type=f32
        ).astype(bf16)
        qpair_copy(k, r, n).start()
        q_keep[k, at] = jnp.dot(grad, head[:, pl.ds(col, width)], preferred_element_type=f32)

    def line_start(k, r):
        @pl.when(peers[r] == z)
        def _():
            q_line[k, z] = q_plane_in[k, place(r)]

        @pl.when(peers[r] != z)
        def _():
            qline_copy(k, r).start()

    def terms_send(k, r, n=1):
        qpair_copy(k, r, n).wait_recv()
        for i in range(r, r + n):
            at = place(i)
            total = (q_keep[k, at] + q_pair_in[k, at].astype(f32)).astype(bf16)
            if i == 0:
                q_plane_in[k, at] = total
                line_start(k, 0)
            else:
                q_plane[k, at] = total
                qplane_copy(k, i).start()

    def terms_line(k):
        for r in (1, 2, 3):
            qplane_copy(k, r).wait_recv()
            line_start(k, r)

    def terms_finish(k):
        for s in range(4):
            @pl.when(s != z)
            def _():
                remote(q_line.at[k, s], q_line.at[k, s], qline_s.at[k, s], qline_r.at[k, s], (g, v)).wait_recv()
        total = q_line[k, 0].astype(f32)
        for s in range(1, 4):
            total = total + q_line[k, s].astype(f32)
        out_hidden[k * rows:(k + 1) * rows, :] = total.astype(bf16)

    def token_columns():
        n = target_ref.shape[1]
        eye = lax.broadcasted_iota(jnp.int32, (n, n), 0) == lax.broadcasted_iota(jnp.int32, (n, n), 1)
        segment = segment_ref[...].astype(f32)
        mask = mask_ref[...].astype(f32)

        def column(row):
            return jnp.sum(jnp.where(eye, row, 0.0), axis=1, keepdims=True)

        counts = jnp.sum(jnp.where(column(segment) == segment, mask, 0.0), axis=1, keepdims=True)
        weights[...] = loss_scale * column(mask) / jnp.maximum(counts, 1.0)
        target_col[...] = column(target_ref[...].astype(f32))

    def stage_a(k):
        hidden_plane(k)
        if k == 0:
            head_copy.wait()
        logits_start(k)

    def stage_d(k):
        grads_start(k)
        terms_start(k, 0)

    def stage_e(k):
        grads_forward(k)
        terms_send(k, 0)
        gat_wait(k, False, 1)
        gat_wait(k, True, 1)
        terms_start(k, 1, 2)

    def stage_f(k):
        gat_wait(k, False, 2)
        gat_wait(k, True, 2)
        terms_start(k, 3)
        terms_send(k, 1, 2)

    def stage_g(k):
        terms_send(k, 3)

    hidden_first(0)
    hidden_first(1)
    token_columns()
    hidden_line(0)
    hidden_first(2)
    hidden_line(1)
    stage_a(0)
    hidden_line(2)
    stage_a(1)
    logits_forward(0)
    stage_a(2)
    logits_forward(1)
    logits_finish(0)
    logits_forward(2)
    stage_d(0)
    logits_finish(1)
    stage_e(0)
    stage_d(1)
    logits_finish(2)
    stage_f(0)
    stage_e(1)
    stage_d(2)
    stage_g(0)
    terms_line(0)
    stage_f(1)
    stage_e(2)
    stage_g(1)
    terms_line(1)
    stage_f(2)
    stage_g(2)
    terms_line(2)

    tiles = 5
    tile_cols = ghead.shape[1] // tiles
    for n in range(tiles):
        at = pl.ds(n * tile_cols, tile_cols)
        total = None
        for k in range(CHUNKS):
            term = lax.dot_general(
                grads[k], mine[k, :, at], (((0,), (0,)), ((), ())), preferred_element_type=f32
            )
            total = term if total is None else total + term
        ghead[:, at] = total.astype(bf16)
    out_copy = pltpu.make_async_copy(ghead, out_head, out_sem)
    out_copy.start()

    for k in range(CHUNKS):
        terms_finish(k)
    for k in range(CHUNKS):
        hidden_finish(k)
        for way in (0, 1):
            for i in (0, 1, 2):
                red_copy(k, way, i).wait_send()
                gat_copy(k, way, i).wait_send()
        for i in range(1, 8):
            stat_copy(k, i).wait_send()
        for r, n in ((0, 1), (1, 2), (3, 1)):
            qpair_copy(k, r, n).wait_send()
        for r in (1, 2, 3):
            qplane_copy(k, r).wait_send()
        for r in range(4):
            @pl.when(peers[r] != z)
            def _():
                qline_copy(k, r).wait_send()
    out_copy.wait()


def fused(hidden, head, targets, segments, loss_mask):
    tokens, width = hidden.shape
    vocab_rows, head_width = head.shape
    rows = tokens // CHUNKS
    half = rows // 2
    bf16, f32 = jnp.bfloat16, jnp.float32
    dma = pltpu.SemaphoreType.DMA
    vmem = pl.BlockSpec(memory_space=pltpu.VMEM)
    hbm = pl.BlockSpec(memory_space=pltpu.HBM)
    anywhere = pl.BlockSpec(memory_space=pl.ANY)
    K = CHUNKS
    return pl.pallas_call(
        functools.partial(kernel, rows, width, vocab_rows),
        out_shape=(
            jax.ShapeDtypeStruct(hidden.shape, bf16),
            jax.ShapeDtypeStruct(head.shape, bf16),
        ),
        in_specs=[hbm, hbm, vmem, vmem, vmem],
        out_specs=(vmem, anywhere),
        scratch_shapes=[
            pltpu.VMEM(head.shape, bf16),
            pltpu.VMEM((K, 4, rows, width), bf16),
            pltpu.VMEM((K, 4 * rows, head_width), bf16),
            pltpu.VMEM((K, 4 * rows, vocab_rows), f32),
            pltpu.VMEM((K, 3, half, vocab_rows), f32),
            pltpu.VMEM((K, 3, half, vocab_rows), f32),
            pltpu.VMEM((128, 128), f32),
            pltpu.VMEM((K, 8, 8, 128), f32),
            pltpu.VMEM((K, 4 * rows, vocab_rows), bf16),
            pltpu.VMEM((tokens, 1), f32),
            pltpu.VMEM((tokens, 1), f32),
            pltpu.VMEM((K, 4 * rows, width), f32),
            pltpu.VMEM((K, 4 * rows, width), bf16),
            pltpu.VMEM((K, 4 * rows, width), bf16),
            pltpu.VMEM((K, 4 * rows, width), bf16),
            pltpu.VMEM((K, 4 * rows, width), bf16),
            pltpu.VMEM((K, 4, rows, width), bf16),
            pltpu.VMEM(head.shape, bf16),
            dma, dma, dma((K,)), dma((K,)),
            dma((K, 2, 3)), dma((K, 2, 3)),
            dma((K, 4)), dma((K, 4)), dma((K, 4)), dma((K, 4)),
            dma((K, 2, 3)), dma((K, 2, 3)),
            dma((K, 7)), dma((K, 7)),
            dma((K, 2, 3)), dma((K, 2, 3)),
            dma((K, 4)), dma((K, 4)), dma((K, 4)), dma((K, 4)), dma((K, 4)), dma((K, 4)),
        ],
        compiler_params=pltpu.CompilerParams(
            collective_id=0, has_side_effects=True, vmem_limit_bytes=40 * 1024 * 1024
        ),
        cost_estimate=pl.CostEstimate(
            flops=3 * 2 * 4 * tokens * vocab_rows * head_width,
            bytes_accessed=4 * vocab_rows * head_width,
            transcendentals=2 * tokens * vocab_rows,
        ),
    )(hidden, head, targets, segments, loss_mask)


def body(hidden, head, targets, segments, loss_mask):
    vocab_rows = head.shape[0]
    features = lax.all_gather(hidden, "vocab", axis=1, tiled=True)
    wide_head = lax.all_gather(head, "dp", axis=1, tiled=True)
    logits = lax.dot_general(
        features, wide_head, (((1,), (1,)), ((), ())), preferred_element_type=jnp.float32
    )
    local_max = jnp.max(logits, axis=1)
    row_max = lax.pmax(local_max, "vocab")
    row_total = lax.psum(jnp.sum(jnp.exp(logits - row_max[:, None]), axis=1), "vocab")
    log_norm = row_max + jnp.log(row_total)
    weight = token_weight(segments, loss_mask)
    vocab_start = lax.axis_index("vocab") * vocab_rows
    columns = vocab_start + lax.broadcasted_iota(jnp.int32, (1, vocab_rows), 1)
    onehot = (targets[0][:, None] == columns).astype(jnp.float32)
    grad_logits = (weight[:, None] * (jnp.exp(logits - log_norm[:, None]) - onehot)).astype(
        jnp.bfloat16
    )
    partial_terms = jnp.dot(grad_logits, wide_head, preferred_element_type=jnp.float32)
    grad_hidden = lax.psum_scatter(partial_terms, "vocab", scatter_dimension=1, tiled=True).astype(
        jnp.bfloat16
    )
    group_cols = lax.all_to_all(features, "dp", split_axis=1, concat_axis=0, tiled=True)
    head_total = lax.dot_general(
        lax.all_gather(grad_logits, "dp", axis=0, tiled=True),
        group_cols,
        (((0,), (0,)), ((), ())),
        preferred_element_type=jnp.float32,
    )
    return (grad_hidden, head_total.astype(jnp.bfloat16))


def solution(mesh):
    placed = (P("dp", "vocab"), P("vocab", "dp"), P("dp", None), P("dp", None), P("dp", None))
    fits = mesh.shape["dp"] == 4 and mesh.shape["vocab"] == 8
    return jax.shard_map(
        fused if fits else body,
        mesh=mesh,
        in_specs=placed,
        out_specs=(P("dp", "vocab"), P("vocab", "dp")),
        check_vma=False,
    )
```

```python
import functools

import jax
import jax.numpy as jnp
from jax import lax
from jax.experimental import pallas as pl
from jax.experimental.pallas import tpu as pltpu
from jax.sharding import PartitionSpec as P

loss_scale = 256.0
MESH = pl.DeviceIdType.MESH
CHUNKS = (1, 2, 2, 1)


def token_weight(segments, loss_mask):
    mask_f = loss_mask[0].astype(jnp.float32)
    seg_ids = segments[0]
    same = (seg_ids[:, None] == seg_ids[None, :]).astype(jnp.float32)
    counts = jnp.sum(same * mask_f[None, :], axis=1)
    return loss_scale * mask_f / jnp.maximum(counts, 1.0)


def kernel(
    sizes, width, vocab_rows,
    hidden_hbm, head_hbm, target_hbm, segment_hbm, mask_hbm,
    out_hidden, out_head,
    head, feats, mine, part, recv_a, recv_b, tile, stats, grads, weights, target_col,
    q_keep, q_pair, q_pair_in, q_plane, q_plane_in, q_line, early, tokens_ref,
    head_sem, token_sem, hidden_sem, own_sem,
    line_s, line_r, plane_s, plane_r, pair_s, pair_r,
    red_s, red_r, stat_s, stat_r, gat_s, gat_r,
    qpair_s, qpair_r, qplane_s, qplane_r, qline_s, qline_r,
):
    g = lax.axis_index("dp")
    v = lax.axis_index("vocab")
    z, c = v // 2, v % 2
    gy, gx = g // 2, g % 2
    xn, yn, dn = gy * 2 + 1 - gx, (1 - gy) * 2 + gx, (1 - gy) * 2 + 1 - gx
    peers = (g, xn, yn, dn)
    sib = z * 2 + 1 - c
    chunks = len(sizes)
    starts = [sum(sizes[:k]) for k in range(chunks)]
    col = pl.multiple_of(c * width, 128)
    other_col = pl.multiple_of((1 - c) * width, 128)
    f32, bf16 = jnp.float32, jnp.bfloat16

    def remote(src, dst, ssem, rsem, dev):
        return pltpu.make_async_remote_copy(
            src_ref=src, dst_ref=dst, send_sem=ssem, recv_sem=rsem,
            device_id=dev, device_id_type=MESH,
        )

    def place(k, r, part=None, bins=1):
        if part is None:
            return pl.ds(r * sizes[k], bins * sizes[k])
        return pl.ds(r * sizes[k] + part * (sizes[k] // 2), sizes[k] // 2)

    def own_rows(k):
        return pl.ds(starts[k], sizes[k])

    def hidden_copy(k):
        return pltpu.make_async_copy(
            hidden_hbm.at[own_rows(k)], feats.at[k, z, pl.ds(0, sizes[k])], hidden_sem.at[k]
        )

    for k in range(chunks):
        hidden_copy(k).start()
    token_copies = [
        pltpu.make_async_copy(ref, tokens_ref.at[i], token_sem.at[i])
        for i, ref in enumerate((target_hbm, segment_hbm, mask_hbm))
    ]
    for copy in token_copies:
        copy.start()
    head_copy = pltpu.make_async_copy(head_hbm, head, head_sem)
    head_copy.start()

    barrier = pltpu.get_barrier_semaphore()
    for p in (xn, yn, dn):
        pl.semaphore_signal(barrier, inc=1, device_id=(p, v), device_id_type=MESH)
    for i in range(1, 8):
        pl.semaphore_signal(barrier, inc=1, device_id=(g, lax.rem(v + i, 8)), device_id_type=MESH)
    tile[...] = jnp.ones_like(tile)
    for k in range(chunks):
        hidden_copy(k).wait()
    pl.semaphore_wait(barrier, 10)

    def line_copy(k, right, d):
        step = 1 if right else -1
        s = z - step * d
        return remote(
            feats.at[k, s, pl.ds(0, sizes[k])], feats.at[k, s, pl.ds(0, sizes[k])], line_s.at[k, int(right), d], line_r.at[k, int(right), d],
            (g, (z + step) * 2 + c),
        )

    def line_ok(right, d):
        if right:
            return (z >= d) & (z < 3)
        return (z + d <= 3) & (z > 0)

    def line_send(k, right, d):
        @pl.when(line_ok(right, d))
        def _():
            line_copy(k, right, d).start()

    def line_send_wait(k, right, d):
        @pl.when(line_ok(right, d))
        def _():
            line_copy(k, right, d).wait_send()

    def plane_copy(k, s):
        r = (gx + s) % 2 + 2 * ((gy + s // 2) % 2)
        at = pl.ds(pl.multiple_of(r * sizes[k], 16), sizes[k])
        return remote(
            feats.at[k, s, pl.ds(0, sizes[k])], mine.at[k, at, pl.ds(col, width)], plane_s.at[k, s], plane_r.at[k, r], (s, v)
        )

    def own_copy(k):
        return pltpu.make_async_copy(
            feats.at[k, g, pl.ds(0, sizes[k])], mine.at[k, place(k, 0), pl.ds(col, width)], own_sem.at[k]
        )

    def plane_send(k, s):
        @pl.when(s == g)
        def _():
            own_copy(k).start()

        @pl.when(s != g)
        def _():
            plane_copy(k, s).start()

    def line_recv(k, right, d):
        step = 1 if right else -1
        s = z - step * d
        here = (z >= d) if right else (z + d <= 3)

        @pl.when(here)
        def _():
            remote(
                feats.at[k, s, pl.ds(0, sizes[k])], feats.at[k, s, pl.ds(0, sizes[k])], line_s.at[k, int(right), d - 1],
                line_r.at[k, int(right), d - 1], (g, v),
            ).wait_recv()
            if d < 3:
                line_send(k, right, d)
            plane_send(k, s)

    def pair_copy(k, r):
        at = mine.at[k, place(k, r), pl.ds(col, width)]
        return remote(at, at, pair_s.at[k, r], pair_r.at[k, r], (g, sib))

    def hidden_first(k):
        line_send(k, True, 0)
        line_send(k, False, 0)
        plane_send(k, z)

    def hidden_line(k):
        for d in (1, 2, 3):
            line_recv(k, True, d)
            line_recv(k, False, d)

    def hidden_plane(k):
        own_copy(k).wait()
        pair_copy(k, 0).start()
        for r in (1, 2, 3):
            at = mine.at[k, place(k, r), pl.ds(col, width)]
            remote(at, at, plane_s.at[k, r], plane_r.at[k, r], (peers[r], v)).wait_recv()
            pair_copy(k, r).start()
        for r in range(4):
            at = mine.at[k, place(k, r), pl.ds(other_col, width)]
            remote(at, at, pair_s.at[k, r], pair_r.at[k, r], (g, sib)).wait_recv()

    def hidden_finish(k):
        for right in (True, False):
            for d in (0, 1, 2):
                line_send_wait(k, right, d)
        for s in range(4):
            @pl.when(s != g)
            def _():
                plane_copy(k, s).wait_send()
        for r in range(4):
            pair_copy(k, r).wait_send()

    def red_copy(k, way, i):
        buf = (recv_a, recv_b)[way]
        first, second = ((1, 2), (2, 1))[way]
        r = (3, first, second)[i]
        dev = peers[(first, first, second)[i]]
        return remote(
            part.at[k, place(k, r, way)], buf.at[k, i, pl.ds(0, sizes[k] // 2)],
            red_s.at[k, way, i], red_r.at[k, way, i], (dev, v),
        )

    def logits_start(k):
        part[k, place(k, 0, bins=4)] = lax.dot_general(
            mine[k, place(k, 0, bins=4)], head[...], (((1,), (1,)), ((), ())), preferred_element_type=f32
        )
        for i in (0, 1):
            for way in (0, 1):
                red_copy(k, way, i).start()

    def logits_forward(k):
        for way in (0, 1):
            buf = (recv_a, recv_b)[way]
            red_copy(k, way, 0).wait_recv()
            at = place(k, (2, 1)[way], way)
            part[k, at] = part[k, at] + buf[k, 0, 0:sizes[k] // 2]
            red_copy(k, way, 2).start()

    def stat_copy(k, i):
        peer = lax.rem(v + i, 8)
        return remote(stats.at[k, v], stats.at[k, v], stat_s.at[k, i - 1], stat_r.at[k, i - 1], (g, peer))

    def logits_finish(k):
        for i in (1, 2):
            for way in (0, 1):
                red_copy(k, way, i).wait_recv()
        for way in (0, 1):
            buf = (recv_a, recv_b)[way]
            at = place(k, 0, way)
            part[k, at] = part[k, at] + buf[k, 1, 0:sizes[k] // 2] + buf[k, 2, 0:sizes[k] // 2]
        logits = part[k, place(k, 0)]
        top = jnp.max(logits, axis=1, keepdims=True)
        total = jnp.sum(jnp.exp(logits - top), axis=1, keepdims=True)
        lane = lax.broadcasted_iota(jnp.int32, (sizes[k], 128), 1)
        tile[0:sizes[k], :] = jnp.where(lane == 0, top, total)
        stats[k, v] = tile[...].T[0:8, :]
        for i in range(1, 8):
            stat_copy(k, i).start()

    def gat_copy(k, to_y, i):
        dev = yn if to_y else xn
        if i == 2:
            src, dst, part_i = (1, 3, 0) if to_y else (2, 3, 1)
        else:
            src, dst, part_i = 0, 2 if to_y else 1, ((1, 0) if to_y else (0, 1))[i]
        return remote(
            grads.at[k, place(k, src, part_i)], grads.at[k, place(k, dst, part_i)],
            gat_s.at[k, int(to_y), i], gat_r.at[k, int(to_y), i], (dev, v),
        )

    def gat_wait(k, to_y, i):
        gat_copy(k, to_y, i).wait_recv()

    def grads_start(k):
        for i in range(1, 8):
            stat_copy(k, i).wait_recv()
        tops = stats[k, :, 0, :]
        totals = stats[k, :, 1, :]
        top = jnp.max(tops, axis=0, keepdims=True)
        total = jnp.sum(totals * jnp.exp(tops - top), axis=0, keepdims=True)
        norm = jnp.broadcast_to(top + jnp.log(total), (128, 128)).T[0:sizes[k], 0:1]
        logits = part[k, place(k, 0)]
        weight = weights[own_rows(k), :]
        target = target_col[own_rows(k), :]
        columns = v * vocab_rows + lax.broadcasted_iota(jnp.int32, (sizes[k], vocab_rows), 1)
        onehot = (target == columns.astype(f32)).astype(f32)
        grads[k, place(k, 0)] = (weight * (jnp.exp(logits - norm) - onehot)).astype(bf16)
        for i in (0, 1):
            for to_y in (False, True):
                gat_copy(k, to_y, i).start()

    def grads_forward(k):
        gat_wait(k, False, 0)
        gat_copy(k, True, 2).start()
        gat_wait(k, True, 0)
        gat_copy(k, False, 2).start()

    def qpair_copy(k, r, n):
        at = place(k, r, bins=n)
        return remote(q_pair.at[k, at], q_pair_in.at[k, at], qpair_s.at[k, r], qpair_r.at[k, r], (g, sib))

    def qplane_copy(k, r):
        return remote(
            q_plane.at[k, place(k, r)], q_plane_in.at[k, place(k, r)], qplane_s.at[k, r], qplane_r.at[k, r], (peers[r], v)
        )

    def qline_copy(k, r):
        s = peers[r]
        return remote(
            q_plane_in.at[k, place(k, r)], q_line.at[k, z, pl.ds(0, sizes[k])], qline_s.at[k, r], qline_r.at[k, z], (g, s * 2 + c)
        )

    def terms_start(k, r, n=1):
        at = place(k, r, bins=n)
        grad = grads[k, at]
        q_pair[k, at] = jnp.dot(
            grad, head[:, pl.ds(other_col, width)], preferred_element_type=f32
        ).astype(bf16)
        qpair_copy(k, r, n).start()
        q_keep[k, at] = jnp.dot(grad, head[:, pl.ds(col, width)], preferred_element_type=f32)

    def line_start(k, r):
        @pl.when(peers[r] == z)
        def _():
            q_line[k, z, 0:sizes[k]] = q_plane_in[k, place(k, r)]

        @pl.when(peers[r] != z)
        def _():
            qline_copy(k, r).start()

    def terms_send(k, r, n=1):
        qpair_copy(k, r, n).wait_recv()
        for i in range(r, r + n):
            at = place(k, i)
            total = (q_keep[k, at] + q_pair_in[k, at].astype(f32)).astype(bf16)
            if i == 0:
                q_plane_in[k, at] = total
                line_start(k, 0)
            else:
                q_plane[k, at] = total
                qplane_copy(k, i).start()

    def terms_line(k):
        for r in (1, 2, 3):
            qplane_copy(k, r).wait_recv()
            line_start(k, r)

    def terms_finish(k):
        for s in range(4):
            @pl.when(s != z)
            def _():
                at = q_line.at[k, s, pl.ds(0, sizes[k])]
                remote(at, at, qline_s.at[k, s], qline_r.at[k, s], (g, v)).wait_recv()
        total = q_line[k, 0, 0:sizes[k]].astype(f32)
        for s in range(1, 4):
            total = total + q_line[k, s, 0:sizes[k]].astype(f32)
        out_hidden[own_rows(k), :] = total.astype(bf16)

    def token_columns():
        for copy in token_copies:
            copy.wait()
        n = tokens_ref.shape[2]
        eye = lax.broadcasted_iota(jnp.int32, (n, n), 0) == lax.broadcasted_iota(jnp.int32, (n, n), 1)
        segment = tokens_ref[1].astype(f32)
        mask = tokens_ref[2].astype(f32)

        def column(row):
            return jnp.sum(jnp.where(eye, row, 0.0), axis=1, keepdims=True)

        counts = jnp.sum(jnp.where(column(segment) == segment, mask, 0.0), axis=1, keepdims=True)
        weights[...] = loss_scale * column(mask) / jnp.maximum(counts, 1.0)
        target_col[...] = column(tokens_ref[0].astype(f32))

    def stage_a(k):
        hidden_plane(k)
        if k == 0:
            head_copy.wait()
        logits_start(k)

    def stage_d(k):
        grads_start(k)
        terms_start(k, 0)

    def stage_e(k):
        grads_forward(k)
        terms_send(k, 0)
        gat_wait(k, False, 1)
        gat_wait(k, True, 1)
        terms_start(k, 1, 2)

    def stage_f(k):
        gat_wait(k, False, 2)
        gat_wait(k, True, 2)
        terms_start(k, 3)
        terms_send(k, 1, 2)

    def stage_g(k):
        terms_send(k, 3)

    def head_term(k, at):
        rows = place(k, 0, bins=4)
        return lax.dot_general(
            grads[k, rows], mine[k, rows, at], (((0,), (0,)), ((), ())), preferred_element_type=f32
        )

    tiles = 5
    tile_cols = out_head.shape[1] // tiles

    def head_early():
        for n in range(tiles):
            at = pl.ds(n * tile_cols, tile_cols)
            total = head_term(0, at)
            for k in range(1, chunks - 1):
                total = total + head_term(k, at)
            early[:, at] = total

    def head_late():
        for n in range(tiles):
            at = pl.ds(n * tile_cols, tile_cols)
            out_head[:, at] = (early[:, at] + head_term(chunks - 1, at)).astype(bf16)

    hidden_first(0)
    hidden_first(1)
    token_columns()
    hidden_line(0)
    for k in range(2, chunks):
        hidden_first(k)
    hidden_line(1)
    steps = (
        (1, logits_forward), (0, stage_a), (3, stage_d), (2, logits_finish),
        (4, stage_e), (5, stage_f), (6, stage_g), (7, terms_line),
    )
    for slot in range(chunks + 7):
        if slot == chunks + 6:
            head_early()
        for lag, step in steps:
            if 0 <= slot - lag < chunks:
                step(slot - lag)
        if slot + 2 < chunks:
            hidden_line(slot + 2)
    head_late()

    for k in range(chunks):
        terms_finish(k)
    for k in range(chunks):
        hidden_finish(k)
        for way in (0, 1):
            for i in (0, 1, 2):
                red_copy(k, way, i).wait_send()
                gat_copy(k, way, i).wait_send()
        for i in range(1, 8):
            stat_copy(k, i).wait_send()
        for r, n in ((0, 1), (1, 2), (3, 1)):
            qpair_copy(k, r, n).wait_send()
        for r in (1, 2, 3):
            qplane_copy(k, r).wait_send()
        for r in range(4):
            @pl.when(peers[r] != z)
            def _():
                qline_copy(k, r).wait_send()


def fused(hidden, head, targets, segments, loss_mask):
    tokens, width = hidden.shape
    vocab_rows, head_width = head.shape
    sizes = [tokens * size // sum(CHUNKS) for size in CHUNKS]
    rows = max(sizes)
    half = rows // 2
    bf16, f32 = jnp.bfloat16, jnp.float32
    dma = pltpu.SemaphoreType.DMA
    vmem = pl.BlockSpec(memory_space=pltpu.VMEM)
    hbm = pl.BlockSpec(memory_space=pltpu.HBM)
    K = len(CHUNKS)
    return pl.pallas_call(
        functools.partial(kernel, sizes, width, vocab_rows),
        out_shape=(
            jax.ShapeDtypeStruct(hidden.shape, bf16),
            jax.ShapeDtypeStruct(head.shape, bf16),
        ),
        in_specs=[hbm] * 5,
        out_specs=(vmem, vmem),
        scratch_shapes=[
            pltpu.VMEM(head.shape, bf16),
            pltpu.VMEM((K, 4, rows, width), bf16),
            pltpu.VMEM((K, 4 * rows, head_width), bf16),
            pltpu.VMEM((K, 4 * rows, vocab_rows), f32),
            pltpu.VMEM((K, 3, half, vocab_rows), f32),
            pltpu.VMEM((K, 3, half, vocab_rows), f32),
            pltpu.VMEM((128, 128), f32),
            pltpu.VMEM((K, 8, 8, 128), f32),
            pltpu.VMEM((K, 4 * rows, vocab_rows), bf16),
            pltpu.VMEM((tokens, 1), f32),
            pltpu.VMEM((tokens, 1), f32),
            pltpu.VMEM((K, 4 * rows, width), f32),
            pltpu.VMEM((K, 4 * rows, width), bf16),
            pltpu.VMEM((K, 4 * rows, width), bf16),
            pltpu.VMEM((K, 4 * rows, width), bf16),
            pltpu.VMEM((K, 4 * rows, width), bf16),
            pltpu.VMEM((K, 4, rows, width), bf16),
            pltpu.VMEM(head.shape, f32),
            pltpu.VMEM((3, 1, tokens), jnp.int32),
            dma, dma((3,)), dma((K,)), dma((K,)),
            dma((K, 2, 3)), dma((K, 2, 3)),
            dma((K, 4)), dma((K, 4)), dma((K, 4)), dma((K, 4)),
            dma((K, 2, 3)), dma((K, 2, 3)),
            dma((K, 7)), dma((K, 7)),
            dma((K, 2, 3)), dma((K, 2, 3)),
            dma((K, 4)), dma((K, 4)), dma((K, 4)), dma((K, 4)), dma((K, 4)), dma((K, 4)),
        ],
        compiler_params=pltpu.CompilerParams(
            collective_id=0, has_side_effects=True, vmem_limit_bytes=40 * 1024 * 1024
        ),
        cost_estimate=pl.CostEstimate(
            flops=3 * 2 * 4 * tokens * vocab_rows * head_width,
            bytes_accessed=4 * vocab_rows * head_width,
            transcendentals=2 * tokens * vocab_rows,
        ),
    )(*[pltpu.with_memory_space_constraint(x, pltpu.HBM) for x in (hidden, head, targets, segments, loss_mask)])


def body(hidden, head, targets, segments, loss_mask):
    vocab_rows = head.shape[0]
    features = lax.all_gather(hidden, "vocab", axis=1, tiled=True)
    wide_head = lax.all_gather(head, "dp", axis=1, tiled=True)
    logits = lax.dot_general(
        features, wide_head, (((1,), (1,)), ((), ())), preferred_element_type=jnp.float32
    )
    local_max = jnp.max(logits, axis=1)
    row_max = lax.pmax(local_max, "vocab")
    row_total = lax.psum(jnp.sum(jnp.exp(logits - row_max[:, None]), axis=1), "vocab")
    log_norm = row_max + jnp.log(row_total)
    weight = token_weight(segments, loss_mask)
    vocab_start = lax.axis_index("vocab") * vocab_rows
    columns = vocab_start + lax.broadcasted_iota(jnp.int32, (1, vocab_rows), 1)
    onehot = (targets[0][:, None] == columns).astype(jnp.float32)
    grad_logits = (weight[:, None] * (jnp.exp(logits - log_norm[:, None]) - onehot)).astype(
        jnp.bfloat16
    )
    partial_terms = jnp.dot(grad_logits, wide_head, preferred_element_type=jnp.float32)
    grad_hidden = lax.psum_scatter(partial_terms, "vocab", scatter_dimension=1, tiled=True).astype(
        jnp.bfloat16
    )
    group_cols = lax.all_to_all(features, "dp", split_axis=1, concat_axis=0, tiled=True)
    head_total = lax.dot_general(
        lax.all_gather(grad_logits, "dp", axis=0, tiled=True),
        group_cols,
        (((0,), (0,)), ((), ())),
        preferred_element_type=jnp.float32,
    )
    return (grad_hidden, head_total.astype(jnp.bfloat16))


def solution(mesh):
    placed = (P("dp", "vocab"), P("vocab", "dp"), P("dp", None), P("dp", None), P("dp", None))
    fits = mesh.shape["dp"] == 4 and mesh.shape["vocab"] == 8
    return jax.shard_map(
        fused if fits else body,
        mesh=mesh,
        in_specs=placed,
        out_specs=(P("dp", "vocab"), P("vocab", "dp")),
        check_vma=False,
    )
```

```python
import functools

import jax
import jax.numpy as jnp
from jax import lax
from jax.experimental import pallas as pl
from jax.experimental.pallas import tpu as pltpu
from jax.sharding import PartitionSpec as P

loss_scale = 256.0
MESH = pl.DeviceIdType.MESH
CHUNKS = (1, 2, 2, 1)


def token_weight(segments, loss_mask):
    mask_f = loss_mask[0].astype(jnp.float32)
    seg_ids = segments[0]
    same = (seg_ids[:, None] == seg_ids[None, :]).astype(jnp.float32)
    counts = jnp.sum(same * mask_f[None, :], axis=1)
    return loss_scale * mask_f / jnp.maximum(counts, 1.0)


def kernel(
    sizes, width, vocab_rows,
    hidden_hbm, head_hbm, target_hbm, segment_hbm, mask_hbm,
    out_hidden, out_head,
    head, head_t, feats, mine, part, recv_a, recv_b, tile, stats, grads, weights, target_col,
    q_keep, q_pair, q_pair_in, q_plane, q_plane_in, q_line, early, tokens_ref,
    head_sem, token_sem, hidden_sem, own_sem,
    line_s, line_r, plane_s, plane_r, pair_s, pair_r,
    red_s, red_r, stat_s, stat_r, gat_s, gat_r,
    qpair_s, qpair_r, qplane_s, qplane_r, qline_s, qline_r,
):
    g = lax.axis_index("dp")
    v = lax.axis_index("vocab")
    z, c = v // 2, v % 2
    gy, gx = g // 2, g % 2
    xn, yn, dn = gy * 2 + 1 - gx, (1 - gy) * 2 + gx, (1 - gy) * 2 + 1 - gx
    peers = (g, xn, yn, dn)
    sib = z * 2 + 1 - c
    chunks = len(sizes)
    starts = [sum(sizes[:k]) for k in range(chunks)]
    col = pl.multiple_of(c * width, 128)
    other_col = pl.multiple_of((1 - c) * width, 128)
    f32, bf16 = jnp.float32, jnp.bfloat16

    def remote(src, dst, ssem, rsem, dev):
        return pltpu.make_async_remote_copy(
            src_ref=src, dst_ref=dst, send_sem=ssem, recv_sem=rsem,
            device_id=dev, device_id_type=MESH,
        )

    def place(k, r, part=None, bins=1):
        if part is None:
            return pl.ds(4 * starts[k] + r * sizes[k], bins * sizes[k])
        return pl.ds(4 * starts[k] + r * sizes[k] + part * (sizes[k] // 2), sizes[k] // 2)

    def own_rows(k):
        return pl.ds(starts[k], sizes[k])

    def hidden_copy(k):
        return pltpu.make_async_copy(
            hidden_hbm.at[own_rows(k)], feats.at[k, z, pl.ds(0, sizes[k])], hidden_sem.at[k]
        )

    for k in range(chunks):
        hidden_copy(k).start()
    token_copies = [
        pltpu.make_async_copy(ref, tokens_ref.at[i], token_sem.at[i])
        for i, ref in enumerate((target_hbm, segment_hbm, mask_hbm))
    ]
    for copy in token_copies:
        copy.start()
    head_copy = pltpu.make_async_copy(head_hbm, head, head_sem)
    head_copy.start()

    barrier = pltpu.get_barrier_semaphore()
    for p in (xn, yn, dn):
        pl.semaphore_signal(barrier, inc=1, device_id=(p, v), device_id_type=MESH)
    for i in range(1, 8):
        pl.semaphore_signal(barrier, inc=1, device_id=(g, lax.rem(v + i, 8)), device_id_type=MESH)
    tile[...] = jnp.ones_like(tile)
    for k in range(chunks):
        hidden_copy(k).wait()
    pl.semaphore_wait(barrier, 10)

    def line_copy(k, right, d):
        step = 1 if right else -1
        s = z - step * d
        return remote(
            feats.at[k, s, pl.ds(0, sizes[k])], feats.at[k, s, pl.ds(0, sizes[k])], line_s.at[k, int(right), d], line_r.at[k, int(right), d],
            (g, (z + step) * 2 + c),
        )

    def line_ok(right, d):
        if right:
            return (z >= d) & (z < 3)
        return (z + d <= 3) & (z > 0)

    def line_send(k, right, d):
        @pl.when(line_ok(right, d))
        def _():
            line_copy(k, right, d).start()

    def line_send_wait(k, right, d):
        @pl.when(line_ok(right, d))
        def _():
            line_copy(k, right, d).wait_send()

    def plane_copy(k, s):
        r = (gx + s) % 2 + 2 * ((gy + s // 2) % 2)
        at = pl.ds(pl.multiple_of(4 * starts[k] + r * sizes[k], 16), sizes[k])
        return remote(
            feats.at[k, s, pl.ds(0, sizes[k])], mine.at[at, pl.ds(col, width)], plane_s.at[k, s], plane_r.at[k, r], (s, v)
        )

    def own_copy(k):
        return pltpu.make_async_copy(
            feats.at[k, g, pl.ds(0, sizes[k])], mine.at[place(k, 0), pl.ds(col, width)], own_sem.at[k]
        )

    def plane_send(k, s):
        @pl.when(s == g)
        def _():
            own_copy(k).start()

        @pl.when(s != g)
        def _():
            plane_copy(k, s).start()

    def line_recv(k, right, d):
        step = 1 if right else -1
        s = z - step * d
        here = (z >= d) if right else (z + d <= 3)

        @pl.when(here)
        def _():
            remote(
                feats.at[k, s, pl.ds(0, sizes[k])], feats.at[k, s, pl.ds(0, sizes[k])], line_s.at[k, int(right), d - 1],
                line_r.at[k, int(right), d - 1], (g, v),
            ).wait_recv()
            if d < 3:
                line_send(k, right, d)
            plane_send(k, s)

    def pair_copy(k, r):
        at = mine.at[place(k, r), pl.ds(col, width)]
        return remote(at, at, pair_s.at[k, r], pair_r.at[k, r], (g, sib))

    def hidden_first(k):
        line_send(k, True, 0)
        line_send(k, False, 0)
        plane_send(k, z)

    def hidden_line(k):
        for d in (1, 2, 3):
            line_recv(k, True, d)
            line_recv(k, False, d)

    def hidden_plane(k):
        own_copy(k).wait()
        pair_copy(k, 0).start()
        for r in (1, 2, 3):
            at = mine.at[place(k, r), pl.ds(col, width)]
            remote(at, at, plane_s.at[k, r], plane_r.at[k, r], (peers[r], v)).wait_recv()
            pair_copy(k, r).start()
        for r in range(4):
            at = mine.at[place(k, r), pl.ds(other_col, width)]
            remote(at, at, pair_s.at[k, r], pair_r.at[k, r], (g, sib)).wait_recv()

    def hidden_finish(k):
        for right in (True, False):
            for d in (0, 1, 2):
                line_send_wait(k, right, d)
        for s in range(4):
            @pl.when(s != g)
            def _():
                plane_copy(k, s).wait_send()
        for r in range(4):
            pair_copy(k, r).wait_send()

    def red_copy(k, way, i):
        buf = (recv_a, recv_b)[way]
        first, second = ((1, 2), (2, 1))[way]
        r = (3, first, second)[i]
        dev = peers[(first, first, second)[i]]
        return remote(
            part.at[place(k, r, way)], buf.at[k, i, pl.ds(0, sizes[k] // 2)],
            red_s.at[k, way, i], red_r.at[k, way, i], (dev, v),
        )

    def logits_start(k):
        part[place(k, 0, bins=4)] = lax.dot_general(
            mine[place(k, 0, bins=4)], head_t[...], (((1,), (0,)), ((), ())), preferred_element_type=f32
        )
        for i in (0, 1):
            for way in (0, 1):
                red_copy(k, way, i).start()

    def logits_forward(k):
        for way in (0, 1):
            buf = (recv_a, recv_b)[way]
            red_copy(k, way, 0).wait_recv()
            at = place(k, (2, 1)[way], way)
            part[at] = part[at] + buf[k, 0, 0:sizes[k] // 2]
            red_copy(k, way, 2).start()

    def stat_copy(k, i):
        peer = lax.rem(v + i, 8)
        return remote(stats.at[k, v], stats.at[k, v], stat_s.at[k, i - 1], stat_r.at[k, i - 1], (g, peer))

    def logits_finish(k):
        for i in (1, 2):
            for way in (0, 1):
                red_copy(k, way, i).wait_recv()
        for way in (0, 1):
            buf = (recv_a, recv_b)[way]
            at = place(k, 0, way)
            part[at] = part[at] + buf[k, 1, 0:sizes[k] // 2] + buf[k, 2, 0:sizes[k] // 2]
        logits = part[place(k, 0)]
        top = jnp.max(logits, axis=1, keepdims=True)
        total = jnp.sum(jnp.exp(logits - top), axis=1, keepdims=True)
        lane = lax.broadcasted_iota(jnp.int32, (sizes[k], 128), 1)
        tile[0:sizes[k], :] = jnp.where(lane == 0, top, total)
        stats[k, v] = tile[...].T[0:8, :]
        for i in range(1, 8):
            stat_copy(k, i).start()

    def gat_copy(k, to_y, i):
        dev = yn if to_y else xn
        if i == 2:
            src, dst, part_i = (1, 3, 0) if to_y else (2, 3, 1)
        else:
            src, dst, part_i = 0, 2 if to_y else 1, ((1, 0) if to_y else (0, 1))[i]
        return remote(
            grads.at[place(k, src, part_i)], grads.at[place(k, dst, part_i)],
            gat_s.at[k, int(to_y), i], gat_r.at[k, int(to_y), i], (dev, v),
        )

    def gat_wait(k, to_y, i):
        gat_copy(k, to_y, i).wait_recv()

    def grads_start(k):
        for i in range(1, 8):
            stat_copy(k, i).wait_recv()
        tops = stats[k, :, 0, :]
        totals = stats[k, :, 1, :]
        top = jnp.max(tops, axis=0, keepdims=True)
        total = jnp.sum(totals * jnp.exp(tops - top), axis=0, keepdims=True)
        norm = jnp.broadcast_to(top + jnp.log(total), (128, 128)).T[0:sizes[k], 0:1]
        logits = part[place(k, 0)]
        weight = weights[own_rows(k), :]
        target = target_col[own_rows(k), :]
        columns = v * vocab_rows + lax.broadcasted_iota(jnp.int32, (sizes[k], vocab_rows), 1)
        onehot = (target == columns.astype(f32)).astype(f32)
        grads[place(k, 0)] = (weight * (jnp.exp(logits - norm) - onehot)).astype(bf16)
        for i in (0, 1):
            for to_y in (False, True):
                gat_copy(k, to_y, i).start()

    def grads_forward(k):
        gat_wait(k, False, 0)
        gat_copy(k, True, 2).start()
        gat_wait(k, True, 0)
        gat_copy(k, False, 2).start()

    def qpair_copy(k, r, n):
        at = place(k, r, bins=n)
        return remote(q_pair.at[at], q_pair_in.at[at], qpair_s.at[k, r], qpair_r.at[k, r], (g, sib))

    def qplane_copy(k, r):
        return remote(
            q_plane.at[place(k, r)], q_plane_in.at[place(k, r)], qplane_s.at[k, r], qplane_r.at[k, r], (peers[r], v)
        )

    def qline_copy(k, r):
        s = peers[r]
        return remote(
            q_plane_in.at[place(k, r)], q_line.at[k, z, pl.ds(0, sizes[k])], qline_s.at[k, r], qline_r.at[k, z], (g, s * 2 + c)
        )

    def terms_start(k, r, n=1):
        at = place(k, r, bins=n)
        grad = grads[at]
        q_pair[at] = jnp.dot(
            grad, head[:, pl.ds(other_col, width)], preferred_element_type=f32
        ).astype(bf16)
        qpair_copy(k, r, n).start()
        q_keep[at] = jnp.dot(grad, head[:, pl.ds(col, width)], preferred_element_type=f32)

    def line_start(k, r):
        @pl.when(peers[r] == z)
        def _():
            q_line[k, z, 0:sizes[k]] = q_plane_in[place(k, r)]

        @pl.when(peers[r] != z)
        def _():
            qline_copy(k, r).start()

    def terms_send(k, r, n=1):
        qpair_copy(k, r, n).wait_recv()
        for i in range(r, r + n):
            at = place(k, i)
            total = (q_keep[at] + q_pair_in[at].astype(f32)).astype(bf16)
            if i == 0:
                q_plane_in[at] = total
                line_start(k, 0)
            else:
                q_plane[at] = total
                qplane_copy(k, i).start()

    def terms_line(k):
        for r in (1, 2, 3):
            qplane_copy(k, r).wait_recv()
            line_start(k, r)

    def terms_finish(k):
        for s in range(4):
            @pl.when(s != z)
            def _():
                at = q_line.at[k, s, pl.ds(0, sizes[k])]
                remote(at, at, qline_s.at[k, s], qline_r.at[k, s], (g, v)).wait_recv()
        total = q_line[k, 0, 0:sizes[k]].astype(f32)
        for s in range(1, 4):
            total = total + q_line[k, s, 0:sizes[k]].astype(f32)
        out_hidden[own_rows(k), :] = total.astype(bf16)

    def token_columns():
        for copy in token_copies:
            copy.wait()
        n = tokens_ref.shape[2]
        eye = lax.broadcasted_iota(jnp.int32, (n, n), 0) == lax.broadcasted_iota(jnp.int32, (n, n), 1)
        segment = tokens_ref[1].astype(f32)
        mask = tokens_ref[2].astype(f32)

        def column(row):
            return jnp.sum(jnp.where(eye, row, 0.0), axis=1, keepdims=True)

        counts = jnp.sum(jnp.where(column(segment) == segment, mask, 0.0), axis=1, keepdims=True)
        weights[...] = loss_scale * column(mask) / jnp.maximum(counts, 1.0)
        target_col[...] = column(tokens_ref[0].astype(f32))

    def stage_a(k):
        hidden_plane(k)
        logits_start(k)

    def stage_terms(k):
        for i in (1, 2):
            gat_wait(k, False, i)
            gat_wait(k, True, i)
        terms_start(k, 0, 4)

    def stage_send(k):
        terms_send(k, 0, 4)

    tiles = (pl.ds(0, vocab_rows // 256 * 128), pl.ds(vocab_rows // 256 * 128, vocab_rows - vocab_rows // 256 * 128))
    last = 4 * starts[-1]

    def head_term(at, rows):
        return lax.dot_general(
            grads[rows, at], mine[rows, :], (((0,), (0,)), ((), ())), preferred_element_type=f32
        )

    def head_early():
        for at in tiles:
            early[at, :] = head_term(at, pl.ds(0, last))

    def head_late():
        for at in tiles:
            out_head[at, :] = (early[at, :] + head_term(at, pl.ds(last, 4 * sizes[-1]))).astype(bf16)

    hidden_first(0)
    hidden_first(1)
    token_columns()
    head_copy.wait()
    for n in range(0, vocab_rows, 128):
        head_t[:, n:n + 128] = head[n:n + 128, :].T
    hidden_line(0)
    for k in range(2, chunks):
        hidden_first(k)
    hidden_line(1)
    steps = (
        (1, logits_forward), (0, stage_a), (4, grads_forward), (3, grads_start),
        (6, stage_send), (7, terms_line), (5, stage_terms), (2, logits_finish),
    )
    for slot in range(chunks + 7):
        if slot == chunks + 6:
            head_early()
        for lag, step in steps:
            if 0 <= slot - lag < chunks:
                step(slot - lag)
        if slot + 2 < chunks:
            hidden_line(slot + 2)
    head_late()

    for k in range(chunks):
        terms_finish(k)
    for k in range(chunks):
        hidden_finish(k)
        for way in (0, 1):
            for i in (0, 1, 2):
                red_copy(k, way, i).wait_send()
                gat_copy(k, way, i).wait_send()
        for i in range(1, 8):
            stat_copy(k, i).wait_send()
        qpair_copy(k, 0, 4).wait_send()
        for r in (1, 2, 3):
            qplane_copy(k, r).wait_send()
        for r in range(4):
            @pl.when(peers[r] != z)
            def _():
                qline_copy(k, r).wait_send()


def fused(hidden, head, targets, segments, loss_mask):
    tokens, width = hidden.shape
    vocab_rows, head_width = head.shape
    sizes = [tokens * size // sum(CHUNKS) for size in CHUNKS]
    rows = max(sizes)
    half = rows // 2
    bf16, f32 = jnp.bfloat16, jnp.float32
    dma = pltpu.SemaphoreType.DMA
    vmem = pl.BlockSpec(memory_space=pltpu.VMEM)
    hbm = pl.BlockSpec(memory_space=pltpu.HBM)
    K = len(CHUNKS)
    return pl.pallas_call(
        functools.partial(kernel, sizes, width, vocab_rows),
        out_shape=(
            jax.ShapeDtypeStruct(hidden.shape, bf16),
            jax.ShapeDtypeStruct(head.shape, bf16),
        ),
        in_specs=[hbm] * 5,
        out_specs=(vmem, vmem),
        scratch_shapes=[
            pltpu.VMEM(head.shape, bf16),
            pltpu.VMEM(head.shape[::-1], bf16),
            pltpu.VMEM((K, 4, rows, width), bf16),
            pltpu.VMEM((4 * tokens, head_width), bf16),
            pltpu.VMEM((4 * tokens, vocab_rows), f32),
            pltpu.VMEM((K, 3, half, vocab_rows), f32),
            pltpu.VMEM((K, 3, half, vocab_rows), f32),
            pltpu.VMEM((128, 128), f32),
            pltpu.VMEM((K, 8, 8, 128), f32),
            pltpu.VMEM((4 * tokens, vocab_rows), bf16),
            pltpu.VMEM((tokens, 1), f32),
            pltpu.VMEM((tokens, 1), f32),
            pltpu.VMEM((4 * tokens, width), f32),
            pltpu.VMEM((4 * tokens, width), bf16),
            pltpu.VMEM((4 * tokens, width), bf16),
            pltpu.VMEM((4 * tokens, width), bf16),
            pltpu.VMEM((4 * tokens, width), bf16),
            pltpu.VMEM((K, 4, rows, width), bf16),
            pltpu.VMEM(head.shape, f32),
            pltpu.VMEM((3, 1, tokens), jnp.int32),
            dma, dma((3,)), dma((K,)), dma((K,)),
            dma((K, 2, 3)), dma((K, 2, 3)),
            dma((K, 4)), dma((K, 4)), dma((K, 4)), dma((K, 4)),
            dma((K, 2, 3)), dma((K, 2, 3)),
            dma((K, 7)), dma((K, 7)),
            dma((K, 2, 3)), dma((K, 2, 3)),
            dma((K, 4)), dma((K, 4)), dma((K, 4)), dma((K, 4)), dma((K, 4)), dma((K, 4)),
        ],
        compiler_params=pltpu.CompilerParams(
            collective_id=0, has_side_effects=True, vmem_limit_bytes=40 * 1024 * 1024
        ),
        cost_estimate=pl.CostEstimate(
            flops=3 * 2 * 4 * tokens * vocab_rows * head_width,
            bytes_accessed=4 * vocab_rows * head_width,
            transcendentals=2 * tokens * vocab_rows,
        ),
    )(*[pltpu.with_memory_space_constraint(x, pltpu.HBM) for x in (hidden, head, targets, segments, loss_mask)])


def body(hidden, head, targets, segments, loss_mask):
    vocab_rows = head.shape[0]
    features = lax.all_gather(hidden, "vocab", axis=1, tiled=True)
    wide_head = lax.all_gather(head, "dp", axis=1, tiled=True)
    logits = lax.dot_general(
        features, wide_head, (((1,), (1,)), ((), ())), preferred_element_type=jnp.float32
    )
    local_max = jnp.max(logits, axis=1)
    row_max = lax.pmax(local_max, "vocab")
    row_total = lax.psum(jnp.sum(jnp.exp(logits - row_max[:, None]), axis=1), "vocab")
    log_norm = row_max + jnp.log(row_total)
    weight = token_weight(segments, loss_mask)
    vocab_start = lax.axis_index("vocab") * vocab_rows
    columns = vocab_start + lax.broadcasted_iota(jnp.int32, (1, vocab_rows), 1)
    onehot = (targets[0][:, None] == columns).astype(jnp.float32)
    grad_logits = (weight[:, None] * (jnp.exp(logits - log_norm[:, None]) - onehot)).astype(
        jnp.bfloat16
    )
    partial_terms = jnp.dot(grad_logits, wide_head, preferred_element_type=jnp.float32)
    grad_hidden = lax.psum_scatter(partial_terms, "vocab", scatter_dimension=1, tiled=True).astype(
        jnp.bfloat16
    )
    group_cols = lax.all_to_all(features, "dp", split_axis=1, concat_axis=0, tiled=True)
    head_total = lax.dot_general(
        lax.all_gather(grad_logits, "dp", axis=0, tiled=True),
        group_cols,
        (((0,), (0,)), ((), ())),
        preferred_element_type=jnp.float32,
    )
    return (grad_hidden, head_total.astype(jnp.bfloat16))


def solution(mesh):
    placed = (P("dp", "vocab"), P("vocab", "dp"), P("dp", None), P("dp", None), P("dp", None))
    fits = mesh.shape["dp"] == 4 and mesh.shape["vocab"] == 8
    return jax.shard_map(
        fused if fits else body,
        mesh=mesh,
        in_specs=placed,
        out_specs=(P("dp", "vocab"), P("vocab", "dp")),
        check_vma=False,
    )
```

```python
import functools

import jax
import jax.numpy as jnp
from jax import lax
from jax.experimental import pallas as pl
from jax.experimental.pallas import tpu as pltpu
from jax.sharding import PartitionSpec as P

loss_scale = 256.0
MESH = pl.DeviceIdType.MESH
CHUNKS = (1, 2, 2, 1)


def token_weight(segments, loss_mask):
    mask_f = loss_mask[0].astype(jnp.float32)
    seg_ids = segments[0]
    same = (seg_ids[:, None] == seg_ids[None, :]).astype(jnp.float32)
    counts = jnp.sum(same * mask_f[None, :], axis=1)
    return loss_scale * mask_f / jnp.maximum(counts, 1.0)


def kernel(
    sizes, width, vocab_rows,
    hidden_hbm, head_hbm, target_hbm, segment_hbm, mask_hbm,
    out_hidden, out_head,
    head, head_t, feats, mine, part, recv_a, recv_b, tile, stats, grads, weights, target_col,
    q_keep, q_pair, q_pair_in, q_plane, q_plane_in, q_line, q_relay, early, tokens_ref,
    head_sem, token_sem, hidden_sem, own_sem,
    line_s, line_r, plane_s, plane_r, pair_s, pair_r,
    red_s, red_r, stat_s, stat_r, gat_s, gat_r,
    qpair_s, qpair_r, qplane_s, qplane_r, qline_s, qline_r, relay_r,
):
    g = lax.axis_index("dp")
    v = lax.axis_index("vocab")
    z, c = v // 2, v % 2
    gy, gx = g // 2, g % 2
    xn, yn, dn = gy * 2 + 1 - gx, (1 - gy) * 2 + gx, (1 - gy) * 2 + 1 - gx
    peers = (g, xn, yn, dn)
    sib = z * 2 + 1 - c
    chunks = len(sizes)
    starts = [sum(sizes[:k]) for k in range(chunks)]
    col = pl.multiple_of(c * width, 128)
    other_col = pl.multiple_of((1 - c) * width, 128)
    f32, bf16 = jnp.float32, jnp.bfloat16

    def remote(src, dst, ssem, rsem, dev):
        return pltpu.make_async_remote_copy(
            src_ref=src, dst_ref=dst, send_sem=ssem, recv_sem=rsem,
            device_id=dev, device_id_type=MESH,
        )

    def place(k, r, part=None, bins=1):
        if part is None:
            return pl.ds(4 * starts[k] + r * sizes[k], bins * sizes[k])
        return pl.ds(4 * starts[k] + r * sizes[k] + part * (sizes[k] // 2), sizes[k] // 2)

    def own_rows(k):
        return pl.ds(starts[k], sizes[k])

    def hidden_copy(k):
        return pltpu.make_async_copy(
            hidden_hbm.at[own_rows(k)], feats.at[k, z, pl.ds(0, sizes[k])], hidden_sem.at[k]
        )

    for k in range(chunks):
        hidden_copy(k).start()
    token_copies = [
        pltpu.make_async_copy(ref, tokens_ref.at[i], token_sem.at[i])
        for i, ref in enumerate((target_hbm, segment_hbm, mask_hbm))
    ]
    for copy in token_copies:
        copy.start()
    head_copy = pltpu.make_async_copy(head_hbm, head, head_sem)
    head_copy.start()

    barrier = pltpu.get_barrier_semaphore()
    for p in (xn, yn, dn):
        pl.semaphore_signal(barrier, inc=1, device_id=(p, v), device_id_type=MESH)
    for i in range(1, 8):
        pl.semaphore_signal(barrier, inc=1, device_id=(g, lax.rem(v + i, 8)), device_id_type=MESH)
    tile[...] = jnp.ones_like(tile)
    for k in range(chunks - 1):
        for s in (0, 3):
            @pl.when(z == 3 - s)
            def _():
                q_line[k, s] = jnp.zeros(q_line.shape[2:], bf16)
    for k in range(chunks):
        hidden_copy(k).wait()
    pl.semaphore_wait(barrier, 10)

    def line_copy(k, right, d):
        step = 1 if right else -1
        s = z - step * d
        return remote(
            feats.at[k, s, pl.ds(0, sizes[k])], feats.at[k, s, pl.ds(0, sizes[k])], line_s.at[k, int(right), d], line_r.at[k, int(right), d],
            (g, (z + step) * 2 + c),
        )

    def line_ok(right, d):
        if right:
            return (z >= d) & (z < 3)
        return (z + d <= 3) & (z > 0)

    def line_send(k, right, d):
        @pl.when(line_ok(right, d))
        def _():
            line_copy(k, right, d).start()

    def line_send_wait(k, right, d):
        @pl.when(line_ok(right, d))
        def _():
            line_copy(k, right, d).wait_send()

    def plane_copy(k, s):
        r = (gx + s) % 2 + 2 * ((gy + s // 2) % 2)
        at = pl.ds(pl.multiple_of(4 * starts[k] + r * sizes[k], 16), sizes[k])
        return remote(
            feats.at[k, s, pl.ds(0, sizes[k])], mine.at[at, pl.ds(col, width)], plane_s.at[k, s], plane_r.at[k, r], (s, v)
        )

    def own_copy(k):
        return pltpu.make_async_copy(
            feats.at[k, g, pl.ds(0, sizes[k])], mine.at[place(k, 0), pl.ds(col, width)], own_sem.at[k]
        )

    def plane_send(k, s):
        @pl.when(s == g)
        def _():
            own_copy(k).start()

        @pl.when(s != g)
        def _():
            plane_copy(k, s).start()

    def line_recv(k, right, d):
        step = 1 if right else -1
        s = z - step * d
        here = (z >= d) if right else (z + d <= 3)

        @pl.when(here)
        def _():
            remote(
                feats.at[k, s, pl.ds(0, sizes[k])], feats.at[k, s, pl.ds(0, sizes[k])], line_s.at[k, int(right), d - 1],
                line_r.at[k, int(right), d - 1], (g, v),
            ).wait_recv()
            if d < 3:
                line_send(k, right, d)
            plane_send(k, s)

    def pair_copy(k, r):
        at = mine.at[place(k, r), pl.ds(col, width)]
        return remote(at, at, pair_s.at[k, r], pair_r.at[k, r], (g, sib))

    def hidden_first(k):
        line_send(k, True, 0)
        line_send(k, False, 0)
        plane_send(k, z)

    def hidden_line(k):
        for d in (1, 2, 3):
            line_recv(k, True, d)
            line_recv(k, False, d)

    def hidden_plane(k):
        own_copy(k).wait()
        pair_copy(k, 0).start()
        for r in (1, 2, 3):
            at = mine.at[place(k, r), pl.ds(col, width)]
            remote(at, at, plane_s.at[k, r], plane_r.at[k, r], (peers[r], v)).wait_recv()
            pair_copy(k, r).start()
        for r in range(4):
            at = mine.at[place(k, r), pl.ds(other_col, width)]
            remote(at, at, pair_s.at[k, r], pair_r.at[k, r], (g, sib)).wait_recv()

    def hidden_finish(k):
        for right in (True, False):
            for d in (0, 1, 2):
                line_send_wait(k, right, d)
        for s in range(4):
            @pl.when(s != g)
            def _():
                plane_copy(k, s).wait_send()
        for r in range(4):
            pair_copy(k, r).wait_send()

    def red_copy(k, way, i):
        buf = (recv_a, recv_b)[way]
        first, second = ((1, 2), (2, 1))[way]
        r = (3, first, second)[i]
        dev = peers[(first, first, second)[i]]
        return remote(
            part.at[place(k, r, way)], buf.at[k, i, pl.ds(0, sizes[k] // 2)],
            red_s.at[k, way, i], red_r.at[k, way, i], (dev, v),
        )

    def logits_start(k):
        part[place(k, 0, bins=4)] = lax.dot_general(
            mine[place(k, 0, bins=4)], head_t[...], (((1,), (0,)), ((), ())), preferred_element_type=f32
        )
        for i in (0, 1):
            for way in (0, 1):
                red_copy(k, way, i).start()

    def logits_forward(k):
        for way in (0, 1):
            buf = (recv_a, recv_b)[way]
            red_copy(k, way, 0).wait_recv()
            at = place(k, (2, 1)[way], way)
            part[at] = part[at] + buf[k, 0, 0:sizes[k] // 2]
            red_copy(k, way, 2).start()

    def stat_copy(k, i):
        peer = lax.rem(v + i, 8)
        return remote(stats.at[k, v], stats.at[k, v], stat_s.at[k, i - 1], stat_r.at[k, i - 1], (g, peer))

    def logits_finish(k):
        for i in (1, 2):
            for way in (0, 1):
                red_copy(k, way, i).wait_recv()
        for way in (0, 1):
            buf = (recv_a, recv_b)[way]
            at = place(k, 0, way)
            part[at] = part[at] + buf[k, 1, 0:sizes[k] // 2] + buf[k, 2, 0:sizes[k] // 2]
        logits = part[place(k, 0)]
        top = jnp.max(logits, axis=1, keepdims=True)
        total = jnp.sum(jnp.exp(logits - top), axis=1, keepdims=True)
        lane = lax.broadcasted_iota(jnp.int32, (sizes[k], 128), 1)
        tile[0:sizes[k], :] = jnp.where(lane == 0, top, total)
        stats[k, v] = tile[...].T[0:8, :]
        for i in range(1, 8):
            stat_copy(k, i).start()

    def gat_copy(k, to_y, i):
        dev = yn if to_y else xn
        if i == 2:
            src, dst, part_i = (1, 3, 0) if to_y else (2, 3, 1)
        else:
            src, dst, part_i = 0, 2 if to_y else 1, ((1, 0) if to_y else (0, 1))[i]
        return remote(
            grads.at[place(k, src, part_i)], grads.at[place(k, dst, part_i)],
            gat_s.at[k, int(to_y), i], gat_r.at[k, int(to_y), i], (dev, v),
        )

    def gat_direct(k, r):
        return remote(
            grads.at[place(k, 0)], grads.at[place(k, r)], gat_s.at[k, 0, r - 1], gat_r.at[k, 0, r - 1], (peers[r], v)
        )

    def gat_wait(k, to_y, i):
        gat_copy(k, to_y, i).wait_recv()

    def grads_start(k):
        for i in range(1, 8):
            stat_copy(k, i).wait_recv()
        tops = stats[k, :, 0, :]
        totals = stats[k, :, 1, :]
        top = jnp.max(tops, axis=0, keepdims=True)
        total = jnp.sum(totals * jnp.exp(tops - top), axis=0, keepdims=True)
        norm = jnp.broadcast_to(top + jnp.log(total), (128, 128)).T[0:sizes[k], 0:1]
        logits = part[place(k, 0)]
        weight = weights[own_rows(k), :]
        target = target_col[own_rows(k), :]
        columns = v * vocab_rows + lax.broadcasted_iota(jnp.int32, (sizes[k], vocab_rows), 1)
        onehot = (target == columns.astype(f32)).astype(f32)
        grads[place(k, 0)] = (weight * (jnp.exp(logits - norm) - onehot)).astype(bf16)
        if k == chunks - 1:
            for r in (3, 1, 2):
                gat_direct(k, r).start()
            return
        for i in (0, 1):
            for to_y in (False, True):
                gat_copy(k, to_y, i).start()

    def grads_forward(k):
        if k == chunks - 1:
            return
        gat_wait(k, False, 0)
        gat_copy(k, True, 2).start()
        gat_wait(k, True, 0)
        gat_copy(k, False, 2).start()

    def qpair_copy(k, r, n):
        at = place(k, r, bins=n)
        return remote(q_pair.at[at], q_pair_in.at[at], qpair_s.at[k, r], qpair_r.at[k, r], (g, sib))

    def qplane_copy(k, r):
        return remote(
            q_plane.at[place(k, r)], q_plane_in.at[place(k, r)], qplane_s.at[k, r], qplane_r.at[k, r], (peers[r], v)
        )

    def qline_copy(k, r):
        s = peers[r]
        return remote(
            q_plane_in.at[place(k, r)], q_line.at[k, z, pl.ds(0, sizes[k])], qline_s.at[k, r], qline_r.at[k, z], (g, s * 2 + c)
        )

    def terms_start(k, r, n=1):
        at = place(k, r, bins=n)
        grad = grads[at]
        q_pair[at] = jnp.dot(
            grad, head[:, pl.ds(other_col, width)], preferred_element_type=f32
        ).astype(bf16)
        qpair_copy(k, r, n).start()
        q_keep[at] = jnp.dot(grad, head[:, pl.ds(col, width)], preferred_element_type=f32)

    def line_start(k, r):
        @pl.when(peers[r] == z)
        def _():
            q_line[k, z, 0:sizes[k]] = q_plane_in[place(k, r)]

        if k == chunks - 1:
            @pl.when(peers[r] != z)
            def _():
                qline_copy(k, r).start()

            return

        s = peers[r]
        far = ((z == 0) & (s == 3)) | ((z == 3) & (s == 0))
        held = ((z == 1) & (s == 3)) | ((z == 2) & (s == 0))

        @pl.when(far)
        def _():
            remote(
                q_plane_in.at[place(k, r)], q_relay.at[k, 0, pl.ds(0, sizes[k])], qline_s.at[k, r], relay_r.at[k],
                (g, (1 + z // 3) * 2 + c),
            ).start()

        @pl.when((s != z) & jnp.logical_not(far | held))
        def _():
            qline_copy(k, r).start()

    def terms_relay(k):
        if k == chunks - 1:
            return
        n = sizes[k]

        @pl.when((z == 1) | (z == 2))
        def _():
            s = 6 - 3 * z
            r = (gx + s) % 2 + 2 * ((gy + s // 2) % 2)
            at = q_relay.at[k, 0, pl.ds(0, n)]
            remote(at, at, qline_s.at[k, r], relay_r.at[k], (g, v)).wait_recv()
            rows = pl.ds(pl.multiple_of(4 * starts[k] + r * n, 16), n)
            q_relay[k, 1, 0:n] = (q_plane_in[rows].astype(f32) + q_relay[k, 0, 0:n].astype(f32)).astype(bf16)
            remote(
                q_relay.at[k, 1, pl.ds(0, n)], q_line.at[k, z, pl.ds(0, n)], qline_s.at[k, r], qline_r.at[k, z],
                (g, s * 2 + c),
            ).start()

    def terms_send(k, r, n=1):
        qpair_copy(k, r, n).wait_recv()
        for i in range(r, r + n):
            at = place(k, i)
            total = (q_keep[at] + q_pair_in[at].astype(f32)).astype(bf16)
            if i == 0:
                q_plane_in[at] = total
                line_start(k, 0)
            else:
                q_plane[at] = total
                qplane_copy(k, i).start()

    def terms_line(k):
        for r in (1, 2, 3):
            qplane_copy(k, r).wait_recv()
            line_start(k, r)

    def terms_finish(k):
        for s in range(4):
            arrives = s != z
            if k < chunks - 1 and s in (0, 3):
                arrives = arrives & (z != 3 - s)

            @pl.when(arrives)
            def _():
                at = q_line.at[k, s, pl.ds(0, sizes[k])]
                remote(at, at, qline_s.at[k, s], qline_r.at[k, s], (g, v)).wait_recv()
        total = q_line[k, 0, 0:sizes[k]].astype(f32)
        for s in range(1, 4):
            total = total + q_line[k, s, 0:sizes[k]].astype(f32)
        out_hidden[own_rows(k), :] = total.astype(bf16)

    def token_columns():
        for copy in token_copies:
            copy.wait()
        n = tokens_ref.shape[2]
        eye = lax.broadcasted_iota(jnp.int32, (n, n), 0) == lax.broadcasted_iota(jnp.int32, (n, n), 1)
        segment = tokens_ref[1].astype(f32)
        mask = tokens_ref[2].astype(f32)

        def column(row):
            return jnp.sum(jnp.where(eye, row, 0.0), axis=1, keepdims=True)

        counts = jnp.sum(jnp.where(column(segment) == segment, mask, 0.0), axis=1, keepdims=True)
        weights[...] = loss_scale * column(mask) / jnp.maximum(counts, 1.0)
        target_col[...] = column(tokens_ref[0].astype(f32))

    def stage_a(k):
        hidden_plane(k)
        logits_start(k)

    def stage_terms(k):
        if k == chunks - 1:
            for r in (1, 2, 3):
                gat_direct(k, r).wait_recv()
        else:
            for i in (1, 2):
                gat_wait(k, False, i)
                gat_wait(k, True, i)
        terms_start(k, 0, 4)

    def stage_send(k):
        terms_send(k, 0, 4)

    tiles = (pl.ds(0, vocab_rows // 256 * 128), pl.ds(vocab_rows // 256 * 128, vocab_rows - vocab_rows // 256 * 128))
    last = 4 * starts[-1]

    def head_term(at, rows):
        return lax.dot_general(
            grads[rows, at], mine[rows, :], (((0,), (0,)), ((), ())), preferred_element_type=f32
        )

    def head_early():
        for at in tiles:
            early[at, :] = head_term(at, pl.ds(0, last))

    def head_late():
        for at in tiles:
            out_head[at, :] = (early[at, :] + head_term(at, pl.ds(last, 4 * sizes[-1]))).astype(bf16)

    hidden_first(0)
    hidden_first(1)
    token_columns()
    head_copy.wait()
    for n in range(0, vocab_rows, 128):
        head_t[:, n:n + 128] = head[n:n + 128, :].T
    hidden_line(0)
    for k in range(2, chunks):
        hidden_first(k)
    hidden_line(1)
    steps = (
        (1, logits_forward), (0, stage_a), (4, grads_forward), (3, grads_start),
        (6, stage_send), (7, terms_line), (8, terms_relay), (5, stage_terms), (2, logits_finish),
    )
    for slot in range(chunks + 7):
        if slot == chunks + 6:
            head_early()
        for lag, step in steps:
            if 0 <= slot - lag < chunks:
                step(slot - lag)
        if slot + 2 < chunks:
            hidden_line(slot + 2)
    head_late()

    for k in range(chunks):
        terms_finish(k)
    for k in range(chunks):
        hidden_finish(k)
        for way in (0, 1):
            for i in (0, 1, 2):
                red_copy(k, way, i).wait_send()
                if k < chunks - 1:
                    gat_copy(k, way, i).wait_send()
        if k == chunks - 1:
            for r in (1, 2, 3):
                gat_direct(k, r).wait_send()
        for i in range(1, 8):
            stat_copy(k, i).wait_send()
        qpair_copy(k, 0, 4).wait_send()
        for r in (1, 2, 3):
            qplane_copy(k, r).wait_send()
        for r in range(4):
            @pl.when(peers[r] != z)
            def _():
                qline_copy(k, r).wait_send()


def fused(hidden, head, targets, segments, loss_mask):
    tokens, width = hidden.shape
    vocab_rows, head_width = head.shape
    sizes = [tokens * size // sum(CHUNKS) for size in CHUNKS]
    rows = max(sizes)
    half = rows // 2
    bf16, f32 = jnp.bfloat16, jnp.float32
    dma = pltpu.SemaphoreType.DMA
    vmem = pl.BlockSpec(memory_space=pltpu.VMEM)
    hbm = pl.BlockSpec(memory_space=pltpu.HBM)
    K = len(CHUNKS)
    return pl.pallas_call(
        functools.partial(kernel, sizes, width, vocab_rows),
        out_shape=(
            jax.ShapeDtypeStruct(hidden.shape, bf16),
            jax.ShapeDtypeStruct(head.shape, bf16),
        ),
        in_specs=[hbm] * 5,
        out_specs=(vmem, vmem),
        scratch_shapes=[
            pltpu.VMEM(head.shape, bf16),
            pltpu.VMEM(head.shape[::-1], bf16),
            pltpu.VMEM((K, 4, rows, width), bf16),
            pltpu.VMEM((4 * tokens, head_width), bf16),
            pltpu.VMEM((4 * tokens, vocab_rows), f32),
            pltpu.VMEM((K, 3, half, vocab_rows), f32),
            pltpu.VMEM((K, 3, half, vocab_rows), f32),
            pltpu.VMEM((128, 128), f32),
            pltpu.VMEM((K, 8, 8, 128), f32),
            pltpu.VMEM((4 * tokens, vocab_rows), bf16),
            pltpu.VMEM((tokens, 1), f32),
            pltpu.VMEM((tokens, 1), f32),
            pltpu.VMEM((4 * tokens, width), f32),
            pltpu.VMEM((4 * tokens, width), bf16),
            pltpu.VMEM((4 * tokens, width), bf16),
            pltpu.VMEM((4 * tokens, width), bf16),
            pltpu.VMEM((4 * tokens, width), bf16),
            pltpu.VMEM((K, 4, rows, width), bf16),
            pltpu.VMEM((K, 2, rows, width), bf16),
            pltpu.VMEM(head.shape, f32),
            pltpu.VMEM((3, 1, tokens), jnp.int32),
            dma, dma((3,)), dma((K,)), dma((K,)),
            dma((K, 2, 3)), dma((K, 2, 3)),
            dma((K, 4)), dma((K, 4)), dma((K, 4)), dma((K, 4)),
            dma((K, 2, 3)), dma((K, 2, 3)),
            dma((K, 7)), dma((K, 7)),
            dma((K, 2, 3)), dma((K, 2, 3)),
            dma((K, 4)), dma((K, 4)), dma((K, 4)), dma((K, 4)), dma((K, 4)), dma((K, 4)), dma((K,)),
        ],
        compiler_params=pltpu.CompilerParams(
            collective_id=0, has_side_effects=True, vmem_limit_bytes=40 * 1024 * 1024
        ),
        cost_estimate=pl.CostEstimate(
            flops=3 * 2 * 4 * tokens * vocab_rows * head_width,
            bytes_accessed=4 * vocab_rows * head_width,
            transcendentals=2 * tokens * vocab_rows,
        ),
    )(*[pltpu.with_memory_space_constraint(x, pltpu.HBM) for x in (hidden, head, targets, segments, loss_mask)])


def body(hidden, head, targets, segments, loss_mask):
    vocab_rows = head.shape[0]
    features = lax.all_gather(hidden, "vocab", axis=1, tiled=True)
    wide_head = lax.all_gather(head, "dp", axis=1, tiled=True)
    logits = lax.dot_general(
        features, wide_head, (((1,), (1,)), ((), ())), preferred_element_type=jnp.float32
    )
    local_max = jnp.max(logits, axis=1)
    row_max = lax.pmax(local_max, "vocab")
    row_total = lax.psum(jnp.sum(jnp.exp(logits - row_max[:, None]), axis=1), "vocab")
    log_norm = row_max + jnp.log(row_total)
    weight = token_weight(segments, loss_mask)
    vocab_start = lax.axis_index("vocab") * vocab_rows
    columns = vocab_start + lax.broadcasted_iota(jnp.int32, (1, vocab_rows), 1)
    onehot = (targets[0][:, None] == columns).astype(jnp.float32)
    grad_logits = (weight[:, None] * (jnp.exp(logits - log_norm[:, None]) - onehot)).astype(
        jnp.bfloat16
    )
    partial_terms = jnp.dot(grad_logits, wide_head, preferred_element_type=jnp.float32)
    grad_hidden = lax.psum_scatter(partial_terms, "vocab", scatter_dimension=1, tiled=True).astype(
        jnp.bfloat16
    )
    group_cols = lax.all_to_all(features, "dp", split_axis=1, concat_axis=0, tiled=True)
    head_total = lax.dot_general(
        lax.all_gather(grad_logits, "dp", axis=0, tiled=True),
        group_cols,
        (((0,), (0,)), ((), ())),
        preferred_element_type=jnp.float32,
    )
    return (grad_hidden, head_total.astype(jnp.bfloat16))


def solution(mesh):
    placed = (P("dp", "vocab"), P("vocab", "dp"), P("dp", None), P("dp", None), P("dp", None))
    fits = mesh.shape["dp"] == 4 and mesh.shape["vocab"] == 8
    return jax.shard_map(
        fused if fits else body,
        mesh=mesh,
        in_specs=placed,
        out_specs=(P("dp", "vocab"), P("vocab", "dp")),
        check_vma=False,
    )
```

```python
import functools

import jax
import jax.numpy as jnp
from jax import lax
from jax.experimental import pallas as pl
from jax.experimental.pallas import tpu as pltpu
from jax.sharding import PartitionSpec as P

loss_scale = 256.0
MESH = pl.DeviceIdType.MESH
CHUNKS = (1, 2, 2, 1)


def token_weight(segments, loss_mask):
    mask_f = loss_mask[0].astype(jnp.float32)
    seg_ids = segments[0]
    same = (seg_ids[:, None] == seg_ids[None, :]).astype(jnp.float32)
    counts = jnp.sum(same * mask_f[None, :], axis=1)
    return loss_scale * mask_f / jnp.maximum(counts, 1.0)


def kernel(
    sizes, width, vocab_rows,
    hidden_hbm, head_hbm, target_hbm, segment_hbm, mask_hbm,
    out_hidden, out_head,
    head, head_t, feats, mine, part, recv_a, recv_b, tile, stats, grads, weights, target_col,
    q_keep, q_pair, q_pair_in, q_plane, q_plane_in, q_line, early, tokens_ref,
    head_sem, token_sem, hidden_sem, own_sem,
    line_s, line_r, plane_s, plane_r, pair_s, pair_r,
    red_s, red_r, stat_s, stat_r, gat_s, gat_r,
    qpair_s, qpair_r, qplane_s, qplane_r, qline_s, qline_r,
):
    g = lax.axis_index("dp")
    v = lax.axis_index("vocab")
    z, c = v // 2, v % 2
    gy, gx = g // 2, g % 2
    xn, yn, dn = gy * 2 + 1 - gx, (1 - gy) * 2 + gx, (1 - gy) * 2 + 1 - gx
    peers = (g, xn, yn, dn)
    sib = z * 2 + 1 - c
    chunks = len(sizes)
    starts = [sum(sizes[:k]) for k in range(chunks)]
    col = pl.multiple_of(c * width, 128)
    other_col = pl.multiple_of((1 - c) * width, 128)
    f32, bf16 = jnp.float32, jnp.bfloat16

    def remote(src, dst, ssem, rsem, dev):
        return pltpu.make_async_remote_copy(
            src_ref=src, dst_ref=dst, send_sem=ssem, recv_sem=rsem,
            device_id=dev, device_id_type=MESH,
        )

    def place(k, r, part=None, bins=1):
        if part is None:
            return pl.ds(4 * starts[k] + r * sizes[k], bins * sizes[k])
        return pl.ds(4 * starts[k] + r * sizes[k] + part * (sizes[k] // 2), sizes[k] // 2)

    def own_rows(k):
        return pl.ds(starts[k], sizes[k])

    def hidden_copy(k):
        return pltpu.make_async_copy(
            hidden_hbm.at[own_rows(k)], feats.at[k, z, pl.ds(0, sizes[k])], hidden_sem.at[k]
        )

    for k in range(chunks):
        hidden_copy(k).start()
    token_copies = [
        pltpu.make_async_copy(ref, tokens_ref.at[i], token_sem.at[i])
        for i, ref in enumerate((target_hbm, segment_hbm, mask_hbm))
    ]
    for copy in token_copies:
        copy.start()
    head_copy = pltpu.make_async_copy(head_hbm, head, head_sem)
    head_copy.start()

    barrier = pltpu.get_barrier_semaphore()
    for p in (xn, yn, dn):
        pl.semaphore_signal(barrier, inc=1, device_id=(p, v), device_id_type=MESH)
    for i in range(1, 8):
        pl.semaphore_signal(barrier, inc=1, device_id=(g, lax.rem(v + i, 8)), device_id_type=MESH)
    tile[...] = jnp.ones_like(tile)
    for k in range(chunks):
        hidden_copy(k).wait()
    pl.semaphore_wait(barrier, 10)

    def line_copy(k, right, d):
        step = 1 if right else -1
        s = z - step * d
        return remote(
            feats.at[k, s, pl.ds(0, sizes[k])], feats.at[k, s, pl.ds(0, sizes[k])], line_s.at[k, int(right), d], line_r.at[k, int(right), d],
            (g, (z + step) * 2 + c),
        )

    def line_ok(right, d):
        if right:
            return (z >= d) & (z < 3)
        return (z + d <= 3) & (z > 0)

    def line_send(k, right, d):
        @pl.when(line_ok(right, d))
        def _():
            line_copy(k, right, d).start()

    def line_send_wait(k, right, d):
        @pl.when(line_ok(right, d))
        def _():
            line_copy(k, right, d).wait_send()

    def plane_copy(k, s):
        r = (gx + s) % 2 + 2 * ((gy + s // 2) % 2)
        at = pl.ds(pl.multiple_of(4 * starts[k] + r * sizes[k], 16), sizes[k])
        return remote(
            feats.at[k, s, pl.ds(0, sizes[k])], mine.at[at, pl.ds(col, width)], plane_s.at[k, s], plane_r.at[k, r], (s, v)
        )

    def own_copy(k):
        return pltpu.make_async_copy(
            feats.at[k, g, pl.ds(0, sizes[k])], mine.at[place(k, 0), pl.ds(col, width)], own_sem.at[k]
        )

    def plane_send(k, s):
        @pl.when(s == g)
        def _():
            own_copy(k).start()

        @pl.when(s != g)
        def _():
            plane_copy(k, s).start()

    def line_recv(k, right, d):
        step = 1 if right else -1
        s = z - step * d
        here = (z >= d) if right else (z + d <= 3)

        @pl.when(here)
        def _():
            remote(
                feats.at[k, s, pl.ds(0, sizes[k])], feats.at[k, s, pl.ds(0, sizes[k])], line_s.at[k, int(right), d - 1],
                line_r.at[k, int(right), d - 1], (g, v),
            ).wait_recv()
            if d < 3:
                line_send(k, right, d)
            plane_send(k, s)

    def pair_copy(k, r):
        at = mine.at[place(k, r), pl.ds(col, width)]
        return remote(at, at, pair_s.at[k, r], pair_r.at[k, r], (g, sib))

    def hidden_first(k):
        line_send(k, True, 0)
        line_send(k, False, 0)
        plane_send(k, z)

    def hidden_line(k, d):
        line_recv(k, True, d)
        line_recv(k, False, d)

    def hidden_plane(k):
        own_copy(k).wait()
        pair_copy(k, 0).start()
        for r in (1, 2, 3):
            at = mine.at[place(k, r), pl.ds(col, width)]
            remote(at, at, plane_s.at[k, r], plane_r.at[k, r], (peers[r], v)).wait_recv()
            pair_copy(k, r).start()
        for r in range(4):
            at = mine.at[place(k, r), pl.ds(other_col, width)]
            remote(at, at, pair_s.at[k, r], pair_r.at[k, r], (g, sib)).wait_recv()

    def hidden_finish(k):
        for right in (True, False):
            for d in (0, 1, 2):
                line_send_wait(k, right, d)
        for s in range(4):
            @pl.when(s != g)
            def _():
                plane_copy(k, s).wait_send()
        for r in range(4):
            pair_copy(k, r).wait_send()

    def red_copy(k, way, i):
        buf = (recv_a, recv_b)[way]
        first, second = ((1, 2), (2, 1))[way]
        r = (3, first, second)[i]
        dev = peers[(first, first, second)[i]]
        return remote(
            part.at[place(k, r, way)], buf.at[k, i, pl.ds(0, sizes[k] // 2)],
            red_s.at[k, way, i], red_r.at[k, way, i], (dev, v),
        )

    def logits_start(k):
        part[place(k, 0, bins=4)] = lax.dot_general(
            mine[place(k, 0, bins=4)], head_t[...], (((1,), (0,)), ((), ())), preferred_element_type=f32
        )
        for i in (0, 1):
            for way in (0, 1):
                red_copy(k, way, i).start()

    def logits_forward(k):
        for way in (0, 1):
            buf = (recv_a, recv_b)[way]
            red_copy(k, way, 0).wait_recv()
            at = place(k, (2, 1)[way], way)
            part[at] = part[at] + buf[k, 0, 0:sizes[k] // 2]
            red_copy(k, way, 2).start()

    def stat_copy(k, i):
        peer = lax.rem(v + i, 8)
        return remote(stats.at[k, v], stats.at[k, v], stat_s.at[k, i - 1], stat_r.at[k, i - 1], (g, peer))

    def logits_finish(k):
        for i in (1, 2):
            for way in (0, 1):
                red_copy(k, way, i).wait_recv()
        for way in (0, 1):
            buf = (recv_a, recv_b)[way]
            at = place(k, 0, way)
            part[at] = part[at] + buf[k, 1, 0:sizes[k] // 2] + buf[k, 2, 0:sizes[k] // 2]
        logits = part[place(k, 0)]
        top = jnp.max(logits, axis=1, keepdims=True)
        total = jnp.sum(jnp.exp(logits - top), axis=1, keepdims=True)
        lane = lax.broadcasted_iota(jnp.int32, (sizes[k], 128), 1)
        tile[0:sizes[k], :] = jnp.where(lane == 0, top, total)
        stats[k, v] = tile[...].T[0:8, :]
        for i in range(1, 8):
            stat_copy(k, i).start()

    def gat_copy(k, to_y, i):
        dev = yn if to_y else xn
        if i == 2:
            src, dst, part_i = (1, 3, 0) if to_y else (2, 3, 1)
        else:
            src, dst, part_i = 0, 2 if to_y else 1, ((1, 0) if to_y else (0, 1))[i]
        return remote(
            grads.at[place(k, src, part_i)], grads.at[place(k, dst, part_i)],
            gat_s.at[k, int(to_y), i], gat_r.at[k, int(to_y), i], (dev, v),
        )

    def gat_wait(k, to_y, i):
        gat_copy(k, to_y, i).wait_recv()

    def grads_start(k):
        for i in range(1, 8):
            stat_copy(k, i).wait_recv()
        tops = stats[k, :, 0, :]
        totals = stats[k, :, 1, :]
        top = jnp.max(tops, axis=0, keepdims=True)
        total = jnp.sum(totals * jnp.exp(tops - top), axis=0, keepdims=True)
        norm = jnp.broadcast_to(top + jnp.log(total), (128, 128)).T[0:sizes[k], 0:1]
        logits = part[place(k, 0)]
        weight = weights[own_rows(k), :]
        target = target_col[own_rows(k), :]
        columns = v * vocab_rows + lax.broadcasted_iota(jnp.int32, (sizes[k], vocab_rows), 1)
        onehot = (target == columns.astype(f32)).astype(f32)
        grads[place(k, 0)] = (weight * (jnp.exp(logits - norm) - onehot)).astype(bf16)
        for i in (0, 1):
            for to_y in (False, True):
                gat_copy(k, to_y, i).start()

    def grads_forward(k):
        gat_wait(k, False, 0)
        gat_copy(k, True, 2).start()
        gat_wait(k, True, 0)
        gat_copy(k, False, 2).start()

    def qpair_copy(k, r, n):
        at = place(k, r, bins=n)
        return remote(q_pair.at[at], q_pair_in.at[at], qpair_s.at[k, r], qpair_r.at[k, r], (g, sib))

    def qplane_copy(k, r):
        return remote(
            q_plane.at[place(k, r)], q_plane_in.at[place(k, r)], qplane_s.at[k, r], qplane_r.at[k, r], (peers[r], v)
        )

    def qline_copy(k, r):
        s = peers[r]
        return remote(
            q_plane_in.at[place(k, r)], q_line.at[k, z, pl.ds(0, sizes[k])], qline_s.at[k, r], qline_r.at[k, z], (g, s * 2 + c)
        )

    def terms_start(k, r, n=1):
        at = place(k, r, bins=n)
        grad = grads[at]
        q_pair[at] = jnp.dot(
            grad, head[:, pl.ds(other_col, width)], preferred_element_type=f32
        ).astype(bf16)
        qpair_copy(k, r, n).start()
        q_keep[at] = jnp.dot(grad, head[:, pl.ds(col, width)], preferred_element_type=f32)

    def line_start(k, r):
        @pl.when(peers[r] == z)
        def _():
            q_line[k, z, 0:sizes[k]] = q_plane_in[place(k, r)]

        @pl.when(peers[r] != z)
        def _():
            qline_copy(k, r).start()

    def terms_send(k, r, n=1):
        qpair_copy(k, r, n).wait_recv()
        for i in range(r, r + n):
            at = place(k, i)
            total = (q_keep[at] + q_pair_in[at].astype(f32)).astype(bf16)
            if i == 0:
                q_plane_in[at] = total
                line_start(k, 0)
            else:
                q_plane[at] = total
                qplane_copy(k, i).start()

    def terms_line(k):
        for r in (1, 2, 3):
            qplane_copy(k, r).wait_recv()
            line_start(k, r)

    def terms_finish(k):
        for s in range(4):
            @pl.when(s != z)
            def _():
                at = q_line.at[k, s, pl.ds(0, sizes[k])]
                remote(at, at, qline_s.at[k, s], qline_r.at[k, s], (g, v)).wait_recv()
        total = q_line[k, 0, 0:sizes[k]].astype(f32)
        for s in range(1, 4):
            total = total + q_line[k, s, 0:sizes[k]].astype(f32)
        out_hidden[own_rows(k), :] = total.astype(bf16)

    def token_columns():
        for copy in token_copies:
            copy.wait()
        n = tokens_ref.shape[2]
        eye = lax.broadcasted_iota(jnp.int32, (n, n), 0) == lax.broadcasted_iota(jnp.int32, (n, n), 1)
        segment = tokens_ref[1].astype(f32)
        mask = tokens_ref[2].astype(f32)

        def column(row):
            return jnp.sum(jnp.where(eye, row, 0.0), axis=1, keepdims=True)

        counts = jnp.sum(jnp.where(column(segment) == segment, mask, 0.0), axis=1, keepdims=True)
        weights[...] = loss_scale * column(mask) / jnp.maximum(counts, 1.0)
        target_col[...] = column(tokens_ref[0].astype(f32))

    def stage_a(k):
        hidden_plane(k)
        logits_start(k)

    def stage_terms(k):
        for i in (1, 2):
            gat_wait(k, False, i)
            gat_wait(k, True, i)
        terms_start(k, 0, 4)

    def stage_send(k):
        terms_send(k, 0, 4)

    tiles = (pl.ds(0, vocab_rows // 256 * 128), pl.ds(vocab_rows // 256 * 128, vocab_rows - vocab_rows // 256 * 128))
    last = 4 * starts[-1]

    def head_term(at, rows):
        return lax.dot_general(
            grads[rows, at], mine[rows, :], (((0,), (0,)), ((), ())), preferred_element_type=f32
        )

    def head_early():
        for at in tiles:
            early[at, :] = head_term(at, pl.ds(0, last))

    def head_late():
        for at in tiles:
            out_head[at, :] = (early[at, :] + head_term(at, pl.ds(last, 4 * sizes[-1]))).astype(bf16)

    def turn(n):
        at = pl.ds(n * 128, 128)
        head_t[:, at] = head[at, :].T

    hidden_first(0)
    hidden_first(1)
    token_columns()
    head_copy.wait()
    pieces = iter(range(vocab_rows // 128))
    for k in (0, 1):
        for d in (1, 2, 3):
            hidden_line(k, d)
            for n in (next(pieces, None),):
                if n is not None:
                    turn(n)
        if k == 0:
            for later in range(2, chunks):
                hidden_first(later)
    for n in pieces:
        turn(n)
    arrivals = {
        (stage_a, 0): ((2, 2),), (logits_forward, 0): ((3, 1),),
        (stage_a, 1): ((2, 3), (3, 2)), (stage_a, 2): ((3, 3),),
    }
    hidden_line(2, 1)
    steps = (
        (1, logits_forward), (0, stage_a), (4, grads_forward), (3, grads_start),
        (6, stage_send), (7, terms_line), (5, stage_terms), (2, logits_finish),
    )
    for slot in range(chunks + 7):
        if slot == chunks + 6:
            head_early()
        for lag, step in steps:
            if 0 <= slot - lag < chunks:
                step(slot - lag)
                for k, d in arrivals.get((step, slot - lag), ()):
                    hidden_line(k, d)
    head_late()

    for k in range(chunks):
        terms_finish(k)
    for k in range(chunks):
        hidden_finish(k)
        for way in (0, 1):
            for i in (0, 1, 2):
                red_copy(k, way, i).wait_send()
                gat_copy(k, way, i).wait_send()
        for i in range(1, 8):
            stat_copy(k, i).wait_send()
        qpair_copy(k, 0, 4).wait_send()
        for r in (1, 2, 3):
            qplane_copy(k, r).wait_send()
        for r in range(4):
            @pl.when(peers[r] != z)
            def _():
                qline_copy(k, r).wait_send()


def fused(hidden, head, targets, segments, loss_mask):
    tokens, width = hidden.shape
    vocab_rows, head_width = head.shape
    sizes = [tokens * size // sum(CHUNKS) for size in CHUNKS]
    rows = max(sizes)
    half = rows // 2
    bf16, f32 = jnp.bfloat16, jnp.float32
    dma = pltpu.SemaphoreType.DMA
    vmem = pl.BlockSpec(memory_space=pltpu.VMEM)
    hbm = pl.BlockSpec(memory_space=pltpu.HBM)
    K = len(CHUNKS)
    return pl.pallas_call(
        functools.partial(kernel, sizes, width, vocab_rows),
        out_shape=(
            jax.ShapeDtypeStruct(hidden.shape, bf16),
            jax.ShapeDtypeStruct(head.shape, bf16),
        ),
        in_specs=[hbm] * 5,
        out_specs=(vmem, vmem),
        scratch_shapes=[
            pltpu.VMEM(head.shape, bf16),
            pltpu.VMEM(head.shape[::-1], bf16),
            pltpu.VMEM((K, 4, rows, width), bf16),
            pltpu.VMEM((4 * tokens, head_width), bf16),
            pltpu.VMEM((4 * tokens, vocab_rows), f32),
            pltpu.VMEM((K, 3, half, vocab_rows), f32),
            pltpu.VMEM((K, 3, half, vocab_rows), f32),
            pltpu.VMEM((128, 128), f32),
            pltpu.VMEM((K, 8, 8, 128), f32),
            pltpu.VMEM((4 * tokens, vocab_rows), bf16),
            pltpu.VMEM((tokens, 1), f32),
            pltpu.VMEM((tokens, 1), f32),
            pltpu.VMEM((4 * tokens, width), f32),
            pltpu.VMEM((4 * tokens, width), bf16),
            pltpu.VMEM((4 * tokens, width), bf16),
            pltpu.VMEM((4 * tokens, width), bf16),
            pltpu.VMEM((4 * tokens, width), bf16),
            pltpu.VMEM((K, 4, rows, width), bf16),
            pltpu.VMEM(head.shape, f32),
            pltpu.VMEM((3, 1, tokens), jnp.int32),
            dma, dma((3,)), dma((K,)), dma((K,)),
            dma((K, 2, 3)), dma((K, 2, 3)),
            dma((K, 4)), dma((K, 4)), dma((K, 4)), dma((K, 4)),
            dma((K, 2, 3)), dma((K, 2, 3)),
            dma((K, 7)), dma((K, 7)),
            dma((K, 2, 3)), dma((K, 2, 3)),
            dma((K, 4)), dma((K, 4)), dma((K, 4)), dma((K, 4)), dma((K, 4)), dma((K, 4)),
        ],
        compiler_params=pltpu.CompilerParams(
            collective_id=0, has_side_effects=True, vmem_limit_bytes=40 * 1024 * 1024
        ),
        cost_estimate=pl.CostEstimate(
            flops=3 * 2 * 4 * tokens * vocab_rows * head_width,
            bytes_accessed=4 * vocab_rows * head_width,
            transcendentals=2 * tokens * vocab_rows,
        ),
    )(*[pltpu.with_memory_space_constraint(x, pltpu.HBM) for x in (hidden, head, targets, segments, loss_mask)])


def body(hidden, head, targets, segments, loss_mask):
    vocab_rows = head.shape[0]
    features = lax.all_gather(hidden, "vocab", axis=1, tiled=True)
    wide_head = lax.all_gather(head, "dp", axis=1, tiled=True)
    logits = lax.dot_general(
        features, wide_head, (((1,), (1,)), ((), ())), preferred_element_type=jnp.float32
    )
    local_max = jnp.max(logits, axis=1)
    row_max = lax.pmax(local_max, "vocab")
    row_total = lax.psum(jnp.sum(jnp.exp(logits - row_max[:, None]), axis=1), "vocab")
    log_norm = row_max + jnp.log(row_total)
    weight = token_weight(segments, loss_mask)
    vocab_start = lax.axis_index("vocab") * vocab_rows
    columns = vocab_start + lax.broadcasted_iota(jnp.int32, (1, vocab_rows), 1)
    onehot = (targets[0][:, None] == columns).astype(jnp.float32)
    grad_logits = (weight[:, None] * (jnp.exp(logits - log_norm[:, None]) - onehot)).astype(
        jnp.bfloat16
    )
    partial_terms = jnp.dot(grad_logits, wide_head, preferred_element_type=jnp.float32)
    grad_hidden = lax.psum_scatter(partial_terms, "vocab", scatter_dimension=1, tiled=True).astype(
        jnp.bfloat16
    )
    group_cols = lax.all_to_all(features, "dp", split_axis=1, concat_axis=0, tiled=True)
    head_total = lax.dot_general(
        lax.all_gather(grad_logits, "dp", axis=0, tiled=True),
        group_cols,
        (((0,), (0,)), ((), ())),
        preferred_element_type=jnp.float32,
    )
    return (grad_hidden, head_total.astype(jnp.bfloat16))


def solution(mesh):
    placed = (P("dp", "vocab"), P("vocab", "dp"), P("dp", None), P("dp", None), P("dp", None))
    fits = mesh.shape["dp"] == 4 and mesh.shape["vocab"] == 8
    return jax.shard_map(
        fused if fits else body,
        mesh=mesh,
        in_specs=placed,
        out_specs=(P("dp", "vocab"), P("vocab", "dp")),
        check_vma=False,
    )
```
